256 devices in a mesh: ens: 8 (over y, core), grid: 32 (over x, z).
Axes of the slice: x: 4, y: 4, z: 8, core: 2. Of those that a mesh axis runs over, the one named last changes fastest.
Arguments:
- mesh_latent: bfloat16 [8, 1024, 1024], P('ens', 'grid'), may hold values from -6 to 6
- grid_feat: bfloat16 [8, 8192, 1024], P('ens', 'grid'), may hold values from -6 to 6
- edges: int32 [8192, 3], P('grid'), may hold values from 0 to 1023, as said below
- target: float32 [8192, 100], P('grid'), may hold values from -6 to 6
- w_query: bfloat16 [1024, 1024], replicated, may hold values from -0.1875 to 0.1875
- w_key: bfloat16 [1024, 1024], replicated, may hold values from -0.1875 to 0.1875
- w_value: bfloat16 [1024, 1024], replicated, may hold values from -0.1875 to 0.1875
- w_out: bfloat16 [1024, 100], replicated, may hold values from -0.1875 to 0.1875
Outputs:
- grad_latent: float32 [8, 1024, 1024], P('ens', 'grid')
- loss: float32 [], replicated
The draws below stay inside these ranges and needn't reach their ends.
Inputs may be any that keep to these rules, and one draw needn't show every extreme that they name: `edges`: A point of region r (points r * 256 to (r + 1) * 256 - 1) links only to mesh nodes from max(r * 32 - 8, 0) to min((r + 1) * 32 + 8, 1024) - 1, and in every region both ends of that range are linked by some point.
All inputs are finite; a program needn't handle non-finite values.
Results may differ from the reference program's by a relative error of at most 0.0096.
Values may be sent and summed in bfloat16 or wider, within the bound.
A program may use at most 64 MiB of HBM per device.

```python
import jax
import jax.numpy as jnp
from jax import lax

D = 1024
HEADS = 16
V = 100
K = 3
HALO = 8
MDEV = 32
P_DEV = 256
MEMBERS = 8
NMESH = 1024
NPTS = 8192


def draw_edges(key, part):
    key = jax.random.fold_in(key, 7)
    position = jnp.arange(NPTS, dtype=jnp.int32)
    region = position // P_DEV
    lower = jnp.maximum(region * MDEV - HALO, 0)
    upper = jnp.minimum((region + 1) * MDEV + HALO, NMESH)
    picked = jax.random.randint(key, (NPTS, K), lower[:, None], upper[:, None], dtype=jnp.int32)
    first = position % P_DEV == 0
    col_zero = jnp.where(first, lower, picked[:, 0])
    col_one = jnp.where(first, upper - 1, picked[:, 1])
    picked = picked.at[:, 0].set(col_zero)
    picked = picked.at[:, 1].set(col_one)
    return picked.astype(jnp.int32)


def levels(key, extent, cuts, least, largest):
    loudness, own = 1.0, jax.random.fold_in(key, 6)
    for dim, shards_of in cuts:
        heights = jnp.exp(jax.random.uniform(jax.random.fold_in(own, dim), (shards_of,), jnp.float32, least / len(cuts), largest / len(cuts)))
        loudness = loudness * jnp.repeat(heights, extent[dim] // shards_of).reshape([-1 if axis == dim else 1 for axis in range(len(extent))])
    return loudness


def centred(rng, dims, deviation, limit, pieces=(), kind=jnp.bfloat16):
    loudness = levels(rng, dims, pieces, -0.22, 0.18) if pieces else 1.0
    entries = jax.random.normal(rng, dims, jnp.float32) * deviation * loudness
    return jnp.minimum(jnp.maximum(entries, -limit), limit).astype(kind)


def setup_inputs(seed: int = 0) -> dict:
    seeds = jax.random.split(jax.random.key(seed), 9)
    return {
        "mesh_latent": centred(seeds[0], (MEMBERS, NMESH, D), 1.0, 6.0, ((0, 8), (1, 32))),
        "grid_feat": centred(seeds[1], (MEMBERS, NPTS, D), 1.0, 6.0, ((0, 8), (1, 32))),
        "edges": draw_edges(jax.random.fold_in(seeds[8], 71), 0),
        "target": centred(seeds[3], (NPTS, V), 1.0, 6.0, ((0, 32),), jnp.float32),
        "w_query": centred(seeds[4], (D, D), D ** -0.5, 0.1875),
        "w_key": centred(seeds[5], (D, D), D ** -0.5, 0.1875),
        "w_value": centred(seeds[6], (D, D), D ** -0.5, 0.1875),
        "w_out": centred(seeds[7], (D, V), D ** -0.5, 0.1875),
    }


DELTA_SQ = 0.01
ALPHA = 0.95

def forward(latent, feats, edges, w_query, w_key, w_value, w_out):
    query = jnp.dot(feats, w_query, preferred_element_type=jnp.float32).astype(jnp.bfloat16)
    keys = jnp.dot(latent, w_key, preferred_element_type=jnp.float32).astype(jnp.bfloat16)
    values = jnp.dot(latent, w_value, preferred_element_type=jnp.float32).astype(jnp.bfloat16)
    points = edges.shape[0]
    width = query.shape[1]
    head_size = width // HEADS
    scale = head_size ** (-0.5)
    q_heads = query.astype(jnp.float32).reshape(points, HEADS, head_size)
    k_heads = keys[edges].astype(jnp.float32).reshape(points, K, HEADS, head_size)
    v_heads = values[edges].astype(jnp.float32).reshape(points, K, HEADS, head_size)
    scores = jnp.einsum('phd,pkhd->pkh', q_heads, k_heads) * scale
    attn = jax.nn.softmax(scores, axis=1)
    context = jnp.einsum('pkh,pkhd->phd', attn, v_heads).reshape(points, width).astype(jnp.bfloat16)
    pred = jnp.dot(context, w_out, preferred_element_type=jnp.float32)
    return (pred, (q_heads, v_heads, attn))

def backward(grad_pred, saved, edges, w_out, nodes):
    q_heads, v_heads, attn = saved
    points, heads, head_size = q_heads.shape
    width = heads * head_size
    scale = head_size ** (-0.5)
    grad_context = jnp.dot(grad_pred, w_out.T, precision=lax.Precision.HIGHEST).reshape(points, heads, head_size)
    grad_values = attn[..., None] * grad_context[:, None]
    grad_attn = jnp.einsum('phd,pkhd->pkh', grad_context, v_heads)
    grad_score = attn * (grad_attn - lax.optimization_barrier(jnp.sum(attn * grad_attn, axis=1, keepdims=True)))
    grad_keys = grad_score[..., None] * q_heads[:, None] * scale
    flat = jnp.concatenate([grad_keys.reshape(-1, width), grad_values.reshape(-1, width)], axis=1)
    return jnp.zeros((nodes, 2 * width), jnp.float32).at[edges.reshape(-1)].add(flat)

def smooth(x):
    return jnp.sqrt(x * x + DELTA_SQ)

def slope(x):
    return x / jnp.sqrt(x * x + DELTA_SQ)

def reference(mesh_latent, grid_feat, edges, target, w_query, w_key, w_value, w_out):
    members = mesh_latent.shape[0]
    nodes = mesh_latent.shape[1]
    width = mesh_latent.shape[2]
    coeff = 1.0 - (1.0 - ALPHA) / members
    preds = []
    for member in range(members):
        pred, saved = forward(mesh_latent[member], grid_feat[member], edges, w_query, w_key, w_value, w_out)
        preds.append(pred)
    objective = jnp.float32(0.0)
    grads = []
    for member in range(members):
        own = preds[member]
        pair_sum = jnp.zeros_like(own)
        pair_slope = jnp.zeros_like(own)
        for other in range(members):
            pair_sum = pair_sum + smooth(own - preds[other])
            pair_slope = pair_slope + slope(own - preds[other])
        objective = objective + jnp.sum(smooth(own - target) / members - coeff / (2.0 * members * (members - 1)) * pair_sum)
        grad_pred = slope(own - target) / members - coeff / (members * (members - 1)) * pair_slope
        pred, saved = forward(mesh_latent[member], grid_feat[member], edges, w_query, w_key, w_value, w_out)
        node_grads = backward(grad_pred, saved, edges, w_out, nodes)
        grad = jnp.dot(node_grads[:, :width], w_key.T, precision=lax.Precision.HIGHEST)
        grad = grad + jnp.dot(node_grads[:, width:], w_value.T, precision=lax.Precision.HIGHEST)
        grads.append(grad)
    loss = objective / (edges.shape[0] * target.shape[1])
    return (jnp.stack(grads), loss)
```

```python
import functools
import math

import jax
import jax.numpy as jnp
from jax import lax
from jax.experimental import pallas as pl
from jax.experimental.pallas import tpu as pltpu
from jax.sharding import PartitionSpec as P

HEADS = 16
HALO = 8
DELTA_SQ = 0.01
ALPHA = 0.95
LOG2E = math.log2(math.e)

MESH = pl.DeviceIdType.MESH
F32 = jnp.float32
BF16 = jnp.bfloat16

RIM = 16
ROWS = 16
GROUP = 256
NT = (((1,), (1,)), ((), ()))
TN = (((0,), (0,)), ((), ()))


def kernel(
    members, regions, deep, npts,
    latent_in, feats_in, edges_in, target_in, wq_in, wk_in, wv_in, wo_in,
    grad_out, loss_out,
    lat, feats, edges, target, wq, wk, wv, wo,
    tpad, wof, won, query, vbd, attn, attn16, pred, got, back_out, back,
    gl, halo, ens_loss, x_loss, z_loss, mine,
    load_sem, rim_send, rim_recv, go_send, go_recv, ret_send, ret_recv,
    halo_send, halo_recv, el_send, el_recv, xl_send, xl_recv, zl_send, zl_recv,
):
    me = lax.axis_index("ens")
    region = lax.axis_index("grid")
    wide = regions // deep
    rx, rz = region // deep, lax.rem(region, deep)
    own_nodes, width = latent_in.shape
    points = feats_in.shape[0]
    variables = wo_in.shape[0]
    window = own_nodes + 2 * HALO
    head_size = width // HEADS
    heads = GROUP // head_size
    groups = width // GROUP
    lower = lax.rem(region + regions - 1, regions)
    upper = lax.rem(region + 1, regions)
    peers = [lax.rem(me + k, members) for k in range(members)]
    x_peers = [lax.rem(rx + k, wide) * deep + rz for k in range(1, wide)]
    z_peers = [rx * deep + lax.rem(rz + k, deep) for k in range(1, deep)]

    def load(src, dst, k):
        copy = pltpu.make_async_copy(src, dst, load_sem.at[k])
        copy.start()
        return copy

    load_lat = load(latent_in, lat.at[pl.ds(RIM, own_nodes)], 0)
    load_feats = load(feats_in, feats, 1)
    load_wq = [
        load(wq_in.at[:, pl.ds(g * GROUP, GROUP)], wq.at[:, pl.ds(g * GROUP, GROUP)], 2 + g)
        for g in range(groups)
    ]
    load_wk = load(wk_in, wk, 6)
    load_wv = load(wv_in, wv, 7)
    load_wo = load(wo_in, wo, 8)
    load_edges = load(edges_in, edges, 9)
    load_target = load(target_in, target, 10)

    barrier = pltpu.get_barrier_semaphore()
    for k in range(1, members):
        pl.semaphore_signal(barrier, inc=1, device_id=(peers[k], region), device_id_type=MESH)
    for r in [lower, upper] + x_peers + z_peers:
        pl.semaphore_signal(barrier, inc=1, device_id=(me, r), device_id_type=MESH)
    load_lat.wait()
    pl.semaphore_wait(barrier, members - 1 + 2 + len(x_peers) + len(z_peers))

    def send(src, dst, send_sem, recv_sem, member, r):
        copy = pltpu.make_async_remote_copy(
            src_ref=src, dst_ref=dst, send_sem=send_sem, recv_sem=recv_sem,
            device_id=(member, r), device_id_type=MESH,
        )
        copy.start()
        return copy

    rims = [
        send(lat.at[pl.ds(RIM, RIM)], lat.at[pl.ds(RIM + own_nodes, RIM)],
             rim_send.at[0], rim_recv.at[0], me, lower),
        send(lat.at[pl.ds(own_nodes, RIM)], lat.at[pl.ds(0, RIM)],
             rim_send.at[1], rim_recv.at[1], me, upper),
    ]

    load_feats.wait()
    for g in range(groups):
        cols = pl.ds(g * GROUP, GROUP)
        load_wq[g].wait()
        query[:, cols] = jnp.dot(
            feats[...], wq[:, cols], preferred_element_type=F32
        ).astype(BF16)

    load_edges.wait()
    links = edges[...] - (region * own_nodes - HALO)
    node = lax.broadcasted_iota(jnp.int32, (window, points), 0)
    count = jnp.zeros((window, points), F32)
    for e in range(edges_in.shape[0]):
        count = count + jnp.where(node == links[e : e + 1, :], 1.0, 0.0)
    linked = count > 0.0
    head_of = lax.broadcasted_iota(jnp.int32, (window, GROUP), 1) // head_size

    def spread(x):
        return jnp.concatenate(
            [jnp.where(head_of == h, x, 0.0) for h in range(heads)], axis=0
        ).astype(BF16)

    def gather(x):
        out = jnp.zeros((window, GROUP), F32)
        for h in range(heads):
            out = jnp.where(head_of == h, x[h * window : (h + 1) * window], out)
        return out

    load_wo.wait()
    load_wk.wait()
    load_wv.wait()
    for rim in rims:
        rim.wait()
    total = jnp.zeros((variables, points), F32)
    scale = head_size ** (-0.5)
    for g in range(groups):
        cols = pl.ds(g * GROUP, GROUP)
        keys = jnp.dot(lat[...], wk[:, cols], preferred_element_type=F32)
        values = jnp.dot(lat[...], wv[:, cols], preferred_element_type=F32)
        kb = spread(keys[RIM - HALO : RIM - HALO + window])
        vb = spread(values[RIM - HALO : RIM - HALO + window])
        vbd[g] = vb
        scores = lax.dot_general(kb, query[:, cols], NT, preferred_element_type=F32)
        for h in range(heads):
            rows = pl.ds(h * window, window)
            s = jnp.where(linked, scores[h * window : (h + 1) * window], -jnp.inf)
            top = jnp.max(s, axis=0, keepdims=True)
            e = count * jnp.exp2((s - top) * (scale * LOG2E))
            a = e * (1.0 / jnp.sum(e, axis=0, keepdims=True))
            attn[g, rows, :] = a
        a16 = attn[g].astype(BF16)
        attn16[g] = a16
        ctx = lax.dot_general(vb, a16, TN, preferred_element_type=F32).astype(BF16)
        total = total + jnp.dot(wo[:, cols], ctx, preferred_element_type=F32)
    pred[...] = jnp.zeros_like(pred)
    pred[pl.ds(0, variables), :] = total

    gone = [
        send(pred.at[pl.ds(pl.multiple_of(peers[k] * ROWS, ROWS), ROWS)], got.at[k],
             go_send.at[k], go_recv.at[k], peers[k], region)
        for k in range(1, members)
    ]
    load_target.wait()
    tpad[...] = jnp.zeros_like(tpad)
    tpad[pl.ds(0, variables), :] = target[...]
    wof[...] = jnp.zeros_like(wof)
    wof[pl.ds(0, variables), :] = wo[...].astype(F32)
    won[...] = wof[...].T.astype(BF16)

    first = pl.multiple_of(me * ROWS, ROWS)
    got[0] = pred[pl.ds(first, ROWS), :]
    for copy in gone:
        copy.wait()

    coeff = 1.0 - (1.0 - ALPHA) / members
    pair = coeff / (members * (members - 1))
    loss_part = jnp.zeros((8, 128), F32)
    for top in range(0, ROWS, 8):
        row = lax.broadcasted_iota(jnp.int32, (8, 128), 0) + first + top
        valid = row < variables
        block_loss = jnp.zeros((8, 128), F32)
        for left in range(0, points, 128):
            at = (pl.ds(top, 8), pl.ds(left, 128))
            goal = tpad[pl.ds(first + top, 8), pl.ds(left, 128)]
            ps = [got[(k,) + at] for k in range(members)]
            slopes = [None] * members
            near = jnp.zeros((8, 128), F32)
            apart = jnp.full((8, 128), 0.5 * members * math.sqrt(DELTA_SQ), F32)
            grads = []
            for i in range(members):
                d = ps[i] - goal
                sq = d * d + DELTA_SQ
                inv = lax.rsqrt(sq)
                near = near + sq * inv
                grads.append(d * inv)
            for i in range(members):
                for j in range(i + 1, members):
                    d = ps[i] - ps[j]
                    sq = d * d + DELTA_SQ
                    inv = lax.rsqrt(sq)
                    apart = apart + sq * inv
                    d = d * inv
                    slopes[i] = d if slopes[i] is None else slopes[i] + d
                    slopes[j] = -d if slopes[j] is None else slopes[j] - d
            block_loss = block_loss + (near * (1.0 / members) - apart * pair)
            for i in range(members):
                back_out[(i,) + at] = (grads[i] * (1.0 / members) - slopes[i] * pair).astype(BF16)
        loss_part = loss_part + jnp.where(valid, block_loss, 0.0)

    returned = []
    for k in range(1, members):
        owner = lax.rem(me + members - k, members)
        returned.append(
            send(back_out.at[k], back.at[pl.ds(first, ROWS)],
                 ret_send.at[k], ret_recv.at[k], owner, region)
        )
    mine[0] = loss_part
    ens_loss[me] = loss_part
    el = [
        send(mine.at[0], ens_loss.at[me], el_send.at[k], el_recv.at[k], peers[k], region)
        for k in range(1, members)
    ]
    back[pl.ds(first, ROWS), :] = back_out[0]
    for copy in returned:
        copy.wait()

    for copy in el:
        copy.wait()
    loss_part = ens_loss[0]
    for k in range(1, members):
        loss_part = loss_part + ens_loss[k]
    mine[1] = loss_part
    x_loss[rx] = loss_part
    xl = [
        send(mine.at[1], x_loss.at[rx], xl_send.at[k], xl_recv.at[k], me, r)
        for k, r in enumerate(x_peers)
    ]

    gk, gv = [], []
    for g in range(groups):
        cols = pl.ds(g * GROUP, GROUP)
        gc = jnp.dot(won[cols, :], back[...], preferred_element_type=F32).astype(BF16)
        ga = jnp.dot(vbd[g], gc, preferred_element_type=F32)
        parts = []
        for h in range(heads):
            a = attn[g, pl.ds(h * window, window), :]
            t = a * ga[h * window : (h + 1) * window]
            parts.append(t - a * jnp.sum(t, axis=0, keepdims=True))
        gs = jnp.concatenate(parts, axis=0).astype(BF16)
        gk.append((gather(jnp.dot(gs, query[:, cols], preferred_element_type=F32)) * scale).astype(BF16))
        gv.append(gather(lax.dot_general(attn16[g], gc, NT, preferred_element_type=F32)).astype(BF16))
    gk = jnp.concatenate(gk, axis=1)
    gv = jnp.concatenate(gv, axis=1)

    for copy in xl:
        copy.wait()
    loss_part = x_loss[0]
    for k in range(1, wide):
        loss_part = loss_part + x_loss[k]
    mine[2] = loss_part
    z_loss[rz] = loss_part
    zl = [
        send(mine.at[2], z_loss.at[rz], zl_send.at[k], zl_recv.at[k], me, r)
        for k, r in enumerate(z_peers)
    ]

    for c in range(width // GROUP):
        cols = pl.ds(c * GROUP, GROUP)
        out = lax.dot_general(gk, wk[cols, :], NT, preferred_element_type=F32)
        gl[:, cols] = out + lax.dot_general(gv, wv[cols, :], NT, preferred_element_type=F32)
    rims = [
        send(gl.at[pl.ds(0, HALO)], halo.at[1], halo_send.at[0], halo_recv.at[0], me, lower),
        send(gl.at[pl.ds(window - HALO, HALO)], halo.at[0], halo_send.at[1], halo_recv.at[1], me, upper),
    ]
    grad_out[pl.ds(HALO, own_nodes - 2 * HALO), :] = gl[pl.ds(2 * HALO, own_nodes - 2 * HALO), :]

    for copy in zl:
        copy.wait()
    loss_part = z_loss[0]
    for k in range(1, deep):
        loss_part = loss_part + z_loss[k]
    loss_out[...] = jnp.sum(loss_part, keepdims=True) * (1.0 / npts)

    for rim in rims:
        rim.wait()
    grad_out[pl.ds(0, HALO), :] = gl[pl.ds(HALO, HALO), :] + halo[0]
    grad_out[pl.ds(own_nodes - HALO, HALO), :] = gl[pl.ds(own_nodes, HALO), :] + halo[1]


def local(members, regions, mesh_latent, grid_feat, edges, target, w_query, w_key, w_value, w_out):
    latent = mesh_latent[0]
    feats = grid_feat[0]
    own_nodes, width = latent.shape
    points, links = edges.shape
    variables = target.shape[1]
    window = own_nodes + 2 * HALO
    deep = math.gcd(regions, 8) if regions > 8 else 2
    wide = regions // deep
    groups = width // GROUP
    stack = window * GROUP // (width // HEADS)
    padded = members * ROWS
    dma = pltpu.SemaphoreType.DMA
    any_space = pl.BlockSpec(memory_space=pltpu.HBM)
    vmem = pl.BlockSpec(memory_space=pltpu.VMEM)
    grad, loss = pl.pallas_call(
        functools.partial(kernel, members, regions, deep, points * regions * variables),
        out_shape=(
            jax.ShapeDtypeStruct((own_nodes, width), F32),
            jax.ShapeDtypeStruct((1, 1), F32),
        ),
        in_specs=[any_space] * 8,
        out_specs=(vmem, vmem),
        scratch_shapes=[
            pltpu.VMEM((own_nodes + 2 * RIM, width), BF16),
            pltpu.VMEM((points, width), BF16),
            pltpu.VMEM((links, points), jnp.int32),
            pltpu.VMEM((variables, points), F32),
            pltpu.VMEM((width, width), BF16),
            pltpu.VMEM((width, width), BF16),
            pltpu.VMEM((width, width), BF16),
            pltpu.VMEM((variables, width), BF16),
            pltpu.VMEM((padded, points), F32),
            pltpu.VMEM((padded, width), F32),
            pltpu.VMEM((width, padded), BF16),
            pltpu.VMEM((points, width), BF16),
            pltpu.VMEM((groups, stack, GROUP), BF16),
            pltpu.VMEM((groups, stack, points), F32),
            pltpu.VMEM((groups, stack, points), BF16),
            pltpu.VMEM((padded, points), F32),
            pltpu.VMEM((members, ROWS, points), F32),
            pltpu.VMEM((members, ROWS, points), BF16),
            pltpu.VMEM((padded, points), BF16),
            pltpu.VMEM((window, width), F32),
            pltpu.VMEM((2, HALO, width), F32),
            pltpu.VMEM((members, 8, 128), F32),
            pltpu.VMEM((wide, 8, 128), F32),
            pltpu.VMEM((deep, 8, 128), F32),
            pltpu.VMEM((3, 8, 128), F32),
            dma((11,)),
            dma((2,)), dma((2,)),
            dma((members,)), dma((members,)),
            dma((members,)), dma((members,)),
            dma((2,)), dma((2,)),
            dma((members,)), dma((members,)),
            dma((wide,)), dma((wide,)),
            dma((deep,)), dma((deep,)),
        ],
        compiler_params=pltpu.CompilerParams(
            collective_id=0, has_side_effects=True, vmem_limit_bytes=48 * 1024 * 1024
        ),
    )(latent, feats, edges.T, target.T, w_query, w_key, w_value, w_out.T)
    return grad[None], loss[0, 0]


def solution(mesh):
    in_specs = (
        P("ens", "grid", None),
        P("ens", "grid", None),
        P("grid", None),
        P("grid", None),
        P(),
        P(),
        P(),
        P(),
    )
    out_specs = (P("ens", "grid", None), P())
    return jax.shard_map(
        functools.partial(local, mesh.shape["ens"], mesh.shape["grid"]),
        mesh=mesh, in_specs=in_specs, out_specs=out_specs, check_vma=False,
    )
```

```python
import functools
import math

import jax
import jax.numpy as jnp
from jax import lax
from jax.experimental import pallas as pl
from jax.experimental.pallas import tpu as pltpu
from jax.sharding import PartitionSpec as P

HEADS = 16
HALO = 8
DELTA_SQ = 0.01
ALPHA = 0.95
LOG2E = math.log2(math.e)

MESH = pl.DeviceIdType.MESH
F32 = jnp.float32
BF16 = jnp.bfloat16

CORES = 2
ROWS = 16
GROUP = 256
NT = (((1,), (1,)), ((), ()))
TN = (((0,), (0,)), ((), ()))


def kernel(
    members, regions, deep, npts,
    latent_in, feats_in, edges_in, target_in, wq_in, wk_in, wv_in, wo_in,
    grad_out, loss_out,
    lat, feats, edges, target, wq, wk, wv, wo,
    kv, rim_out, rim_in, tpad, wof, won, query, kbd, vbd, attn, attn16, pred, got, back_out, back,
    gl, halo, plane_loss, deep_loss, mine,
    hello, load_sem, rim_send, rim_recv, go_send, go_recv, ret_send, ret_recv,
    halo_send, halo_recv, pl_send, pl_recv, dl_send, dl_recv,
):
    me = lax.axis_index("ens")
    region = lax.axis_index("grid")
    wide, tall = regions // deep, members // CORES
    rx, rz = region // deep, lax.rem(region, deep)
    ry, rc = me // CORES, lax.rem(me, CORES)
    own_nodes, width = latent_in.shape
    points = feats_in.shape[0]
    variables = wo_in.shape[0]
    window = own_nodes + 2 * HALO
    head_size = width // HEADS
    heads = GROUP // head_size
    groups = width // GROUP
    lower = lax.rem(region + regions - 1, regions)
    upper = lax.rem(region + 1, regions)
    peers = [lax.rem(me + k, members) for k in range(members)]
    plane, line = [], []
    for i in range(1, wide * tall):
        x, y = lax.rem(rx + i // tall, wide), lax.rem(ry + i % tall, tall)
        plane.append((i // tall, y * CORES + rc, x * deep + rz))
    for i in range(1, deep * CORES):
        z, c = lax.rem(rz + i // CORES, deep), lax.rem(rc + i % CORES, CORES)
        line.append((i // CORES, ry * CORES + c, rx * deep + z))

    def load(src, dst, k):
        copy = pltpu.make_async_copy(src, dst, load_sem.at[k])
        copy.start()
        return copy

    def load_columns(src, dst, k):
        return [
            load(src.at[:, pl.ds(g * GROUP, GROUP)], dst.at[:, pl.ds(g * GROUP, GROUP)], k + g)
            for g in range(groups)
        ]

    barrier = pltpu.get_barrier_semaphore()
    near = [
        (ry * CORES + c, rx * deep + lax.rem(rz + step, deep)) for step in (1, deep - 1, 2, deep - 2) for c in range(CORES)
    ]
    greet = [(me, lower), (me, upper)] + near + [(peers[k], region) for k in range(1, members)]
    greet += [(me, lax.rem(rx + k, wide) * deep + rz) for k in range(1, wide)]
    for device in greet:
        pl.semaphore_signal(barrier, inc=1, device_id=device, device_id_type=MESH)

    load_lat = load(latent_in, lat, 0)
    load_wk = load_columns(wk_in, wk, 1)
    load_wv = load_columns(wv_in, wv, 5)
    load_feats = load(feats_in, feats, 9)
    load_wq = load_columns(wq_in, wq, 10)
    load_edges = load(edges_in, edges, 14)
    load_wo = load(wo_in, wo, 15)
    load_target = load(target_in, target, 16)

    def send(src, dst, send_sem, recv_sem, member, r):
        copy = pltpu.make_async_remote_copy(
            src_ref=src, dst_ref=dst, send_sem=send_sem, recv_sem=recv_sem,
            device_id=(member, r), device_id_type=MESH,
        )
        copy.start()
        return copy

    load_lat.wait()
    for g in range(groups):
        cols = pl.ds(g * GROUP, GROUP)
        for i, (loads, w) in enumerate(((load_wk, wk), (load_wv, wv))):
            loads[g].wait()
            kv[i, :, cols] = jnp.dot(lat[...], w[:, cols], preferred_element_type=F32)
    for side, row in enumerate((0, own_nodes - HALO)):
        rim_out[side] = jnp.concatenate(
            [kv[0, pl.ds(row, HALO), :], kv[1, pl.ds(row, HALO), :]], axis=0
        ).astype(BF16)
    pl.semaphore_wait(barrier, len(greet))
    rims = [
        send(rim_out.at[0], rim_in.at[1], rim_send.at[0], rim_recv.at[0], me, lower),
        send(rim_out.at[1], rim_in.at[0], rim_send.at[1], rim_recv.at[1], me, upper),
    ]
    for device in near[len(near) // 2 :]:
        pl.semaphore_signal(hello, inc=1, device_id=device, device_id_type=MESH)

    load_feats.wait()
    for g in range(groups):
        cols = pl.ds(g * GROUP, GROUP)
        load_wq[g].wait()
        query[:, cols] = jnp.dot(
            feats[...], wq[:, cols], preferred_element_type=F32
        ).astype(BF16)

    load_edges.wait()
    links = edges[...] - region * own_nodes
    links = jnp.where(links < 0, links + window, links)
    node = lax.broadcasted_iota(jnp.int32, (window, points), 0)
    node = jnp.where(node < own_nodes, node, jnp.where(node < own_nodes + HALO, node + HALO, node - HALO))
    count = jnp.zeros((window, points), F32)
    for e in range(edges_in.shape[0]):
        count = count + jnp.where(node == links[e : e + 1, :], 1.0, 0.0)
    linked = count > 0.0

    def head_of(rows):
        return lax.broadcasted_iota(jnp.int32, (rows, GROUP), 1) // head_size

    def spread(x, h):
        return jnp.where(head_of(x.shape[0]) == h, x, 0.0).astype(BF16)

    def gather(x):
        out = jnp.zeros((window, GROUP), F32)
        for h in range(heads):
            out = jnp.where(head_of(window) == h, x[h * window : (h + 1) * window], out)
        return out

    for g in range(groups):
        for h in range(heads):
            for i, dst in enumerate((kbd, vbd)):
                dst[g, pl.ds(h * window, own_nodes), :] = spread(kv[i, :, pl.ds(g * GROUP, GROUP)], h)

    load_target.wait()
    load_wo.wait()
    tpad[...] = jnp.zeros_like(tpad)
    tpad[pl.ds(0, variables), :] = target[...]
    wof[...] = jnp.zeros_like(wof)
    wof[pl.ds(0, variables), :] = wo[...].astype(F32)
    won[...] = wof[...].T.astype(BF16)
    pred[...] = jnp.zeros_like(pred)

    for rim in rims:
        rim.wait()
    for i, dst in enumerate((kbd, vbd)):
        for g in range(groups):
            cols = pl.ds(g * GROUP, GROUP)
            both = jnp.concatenate(
                [rim_in[side, :, cols].astype(F32)[i * HALO : (i + 1) * HALO] for side in range(2)], axis=0
            )
            for h in range(heads):
                dst[g, pl.ds(h * window + own_nodes, 2 * HALO), :] = spread(both, h)
    total = jnp.zeros((variables, points), F32)
    scale = head_size ** (-0.5)
    for g in range(groups):
        cols = pl.ds(g * GROUP, GROUP)
        scores = lax.dot_general(kbd[g], query[:, cols], NT, preferred_element_type=F32)
        parts = []
        for h in range(heads):
            s = jnp.where(linked, scores[h * window : (h + 1) * window], -jnp.inf)
            top = jnp.max(s, axis=0, keepdims=True)
            e = count * jnp.exp2((s - top) * (scale * LOG2E))
            a = e * (1.0 / jnp.sum(e, axis=0, keepdims=True))
            attn[g, pl.ds(h * window, window), :] = a
            parts.append(a.astype(BF16))
        a16 = jnp.concatenate(parts, axis=0)
        attn16[g] = a16
        ctx = lax.dot_general(vbd[g], a16, TN, preferred_element_type=F32).astype(BF16)
        total = total + jnp.dot(wo[:, cols], ctx, preferred_element_type=F32)
    pred[pl.ds(0, variables), :] = total

    gone = [
        send(pred.at[pl.ds(pl.multiple_of(peers[k] * ROWS, ROWS), ROWS)], got.at[k],
             go_send.at[k], go_recv.at[k], peers[k], region)
        for k in range(1, members)
    ]
    first = pl.multiple_of(me * ROWS, ROWS)
    got[0] = pred[pl.ds(first, ROWS), :]
    for copy in gone:
        copy.wait()

    coeff = 1.0 - (1.0 - ALPHA) / members
    pair = coeff / (members * (members - 1))
    loss_part = jnp.zeros((8, 128), F32)
    for top in range(0, ROWS, 8):
        row = lax.broadcasted_iota(jnp.int32, (8, 128), 0) + first + top
        valid = row < variables
        block_loss = jnp.zeros((8, 128), F32)
        for left in range(0, points, 128):
            at = (pl.ds(top, 8), pl.ds(left, 128))
            goal = tpad[pl.ds(first + top, 8), pl.ds(left, 128)]
            ps = [got[(k,) + at] for k in range(members)]
            slopes = [None] * members
            near = jnp.zeros((8, 128), F32)
            apart = jnp.full((8, 128), 0.5 * members * math.sqrt(DELTA_SQ), F32)
            grads = []
            for i in range(members):
                d = ps[i] - goal
                sq = d * d + DELTA_SQ
                inv = lax.rsqrt(sq)
                near = near + sq * inv
                grads.append(d * inv)
            for i in range(members):
                for j in range(i + 1, members):
                    d = ps[i] - ps[j]
                    sq = d * d + DELTA_SQ
                    inv = lax.rsqrt(sq)
                    apart = apart + sq * inv
                    d = d * inv
                    slopes[i] = d if slopes[i] is None else slopes[i] + d
                    slopes[j] = -d if slopes[j] is None else slopes[j] - d
            block_loss = block_loss + (near * (1.0 / members) - apart * pair)
            for i in range(members):
                back_out[(i,) + at] = (grads[i] * (1.0 / members) - slopes[i] * pair).astype(BF16)
        loss_part = loss_part + jnp.where(valid, block_loss, 0.0)

    loss_part = jnp.sum(loss_part, axis=0, keepdims=True)
    mine[0] = loss_part
    slot = rx * tall + ry
    plane_loss[slot] = loss_part
    plane_sent = [
        send(mine.at[0], plane_loss.at[slot], pl_send.at[k], pl_recv.at[k], m, r)
        for k, (_, m, r) in enumerate(plane)
    ]
    returned = []
    for k in range(1, members):
        owner = lax.rem(me + members - k, members)
        returned.append(
            send(back_out.at[k], back.at[pl.ds(first, ROWS)],
                 ret_send.at[k], ret_recv.at[k], owner, region)
        )
    back[pl.ds(first, ROWS), :] = back_out[0]
    for copy in returned:
        copy.wait()

    gk, gv = [], []
    for g in range(groups):
        cols = pl.ds(g * GROUP, GROUP)
        gc = jnp.dot(won[cols, :], back[...], preferred_element_type=F32).astype(BF16)
        ga = jnp.dot(vbd[g], gc, preferred_element_type=F32)
        parts = []
        for h in range(heads):
            a = attn[g, pl.ds(h * window, window), :]
            t = a * ga[h * window : (h + 1) * window]
            parts.append(t - a * jnp.sum(t, axis=0, keepdims=True))
        gs = jnp.concatenate(parts, axis=0).astype(BF16)
        gk.append((gather(jnp.dot(gs, query[:, cols], preferred_element_type=F32)) * scale).astype(BF16))
        gv.append(gather(lax.dot_general(attn16[g], gc, NT, preferred_element_type=F32)).astype(BF16))
        if g == 1:
            pl.semaphore_wait(hello, len(near) // 2)
            for copy in plane_sent:
                copy.wait()
            loss_part = plane_loss[0]
            for k in range(1, wide * tall):
                loss_part = loss_part + plane_loss[k]
            mine[1] = loss_part
            slot = rz * CORES + rc
            deep_loss[slot] = loss_part
            line_sent = [
                send(mine.at[1], deep_loss.at[slot], dl_send.at[k], dl_recv.at[k], m, r)
                for k, (_, m, r) in enumerate(line)
            ]
    gk = jnp.concatenate(gk, axis=1)
    gv = jnp.concatenate(gv, axis=1)

    for c in range(width // GROUP):
        cols = pl.ds(c * GROUP, GROUP)
        out = lax.dot_general(gk, wk[cols, :], NT, preferred_element_type=F32)
        gl[:, cols] = out + lax.dot_general(gv, wv[cols, :], NT, preferred_element_type=F32)
    rims = [
        send(gl.at[pl.ds(own_nodes, HALO)], halo.at[1], halo_send.at[0], halo_recv.at[0], me, lower),
        send(gl.at[pl.ds(own_nodes + HALO, HALO)], halo.at[0], halo_send.at[1], halo_recv.at[1], me, upper),
    ]
    grad_out[pl.ds(HALO, own_nodes - 2 * HALO), :] = gl[pl.ds(HALO, own_nodes - 2 * HALO), :]

    for rim in rims:
        rim.wait()
    grad_out[pl.ds(0, HALO), :] = gl[pl.ds(0, HALO), :] + halo[0]
    grad_out[pl.ds(own_nodes - HALO, HALO), :] = gl[pl.ds(own_nodes - HALO, HALO), :] + halo[1]

    for copy in line_sent:
        copy.wait()
    loss_part = deep_loss[0]
    for k in range(1, deep * CORES):
        loss_part = loss_part + deep_loss[k]
    loss_out[...] = jnp.sum(loss_part, keepdims=True) * (1.0 / npts)


def local(members, regions, mesh_latent, grid_feat, edges, target, w_query, w_key, w_value, w_out):
    latent = mesh_latent[0]
    feats = grid_feat[0]
    own_nodes, width = latent.shape
    points, links = edges.shape
    variables = target.shape[1]
    window = own_nodes + 2 * HALO
    deep = math.gcd(regions, 8) if regions > 8 else 2
    wide, tall = regions // deep, members // CORES
    groups = width // GROUP
    stack = window * GROUP // (width // HEADS)
    padded = members * ROWS
    dma = pltpu.SemaphoreType.DMA
    any_space = pl.BlockSpec(memory_space=pltpu.HBM)
    vmem = pl.BlockSpec(memory_space=pltpu.VMEM)
    grad, loss = pl.pallas_call(
        functools.partial(kernel, members, regions, deep, points * regions * variables),
        out_shape=(
            jax.ShapeDtypeStruct((own_nodes, width), F32),
            jax.ShapeDtypeStruct((1, 1), F32),
        ),
        in_specs=[any_space] * 8,
        out_specs=(vmem, vmem),
        scratch_shapes=[
            pltpu.VMEM((own_nodes, width), BF16),
            pltpu.VMEM((points, width), BF16),
            pltpu.VMEM((links, points), jnp.int32),
            pltpu.VMEM((variables, points), F32),
            pltpu.VMEM((width, width), BF16),
            pltpu.VMEM((width, width), BF16),
            pltpu.VMEM((width, width), BF16),
            pltpu.VMEM((variables, width), BF16),
            pltpu.VMEM((2, own_nodes, width), F32),
            pltpu.VMEM((2, 2 * HALO, width), BF16),
            pltpu.VMEM((2, 2 * HALO, width), BF16),
            pltpu.VMEM((padded, points), F32),
            pltpu.VMEM((padded, width), F32),
            pltpu.VMEM((width, padded), BF16),
            pltpu.VMEM((points, width), BF16),
            pltpu.VMEM((groups, stack, GROUP), BF16),
            pltpu.VMEM((groups, stack, GROUP), BF16),
            pltpu.VMEM((groups, stack, points), F32),
            pltpu.VMEM((groups, stack, points), BF16),
            pltpu.VMEM((padded, points), F32),
            pltpu.VMEM((members, ROWS, points), F32),
            pltpu.VMEM((members, ROWS, points), BF16),
            pltpu.VMEM((padded, points), BF16),
            pltpu.VMEM((window, width), F32),
            pltpu.VMEM((2, HALO, width), F32),
            pltpu.VMEM((wide * tall, 1, 128), F32),
            pltpu.VMEM((deep * CORES, 1, 128), F32),
            pltpu.VMEM((2, 1, 128), F32),
            pltpu.SemaphoreType.REGULAR,
            dma((17,)),
            dma((2,)), dma((2,)),
            dma((members,)), dma((members,)),
            dma((members,)), dma((members,)),
            dma((2,)), dma((2,)),
            dma((wide * tall,)), dma((wide * tall,)),
            dma((deep * CORES,)), dma((deep * CORES,)),
        ],
        compiler_params=pltpu.CompilerParams(
            collective_id=0, has_side_effects=True, vmem_limit_bytes=24 * 1024 * 1024
        ),
    )(*[pltpu.with_memory_space_constraint(x, pltpu.HBM) for x in (latent, feats, edges.T, target.T, w_query, w_key, w_value, w_out.T)])
    return grad[None], loss[0, 0]


def solution(mesh):
    in_specs = (
        P("ens", "grid", None),
        P("ens", "grid", None),
        P("grid", None),
        P("grid", None),
        P(),
        P(),
        P(),
        P(),
    )
    out_specs = (P("ens", "grid", None), P())
    return jax.shard_map(
        functools.partial(local, mesh.shape["ens"], mesh.shape["grid"]),
        mesh=mesh, in_specs=in_specs, out_specs=out_specs, check_vma=False,
    )
```

```python
import functools
import math

import jax
import jax.numpy as jnp
from jax import lax
from jax.experimental import pallas as pl
from jax.experimental.pallas import tpu as pltpu
from jax.sharding import PartitionSpec as P

HEADS = 16
HALO = 8
DELTA_SQ = 0.01
ALPHA = 0.95
LOG2E = math.log2(math.e)

MESH = pl.DeviceIdType.MESH
F32 = jnp.float32
BF16 = jnp.bfloat16

CORES = 2
ROWS = 16
GROUP = 256
NT = (((1,), (1,)), ((), ()))
TN = (((0,), (0,)), ((), ()))


def kernel(
    members, regions, deep, npts,
    latent_in, feats_in, edges_in, target_in, wq_in, wk_in, wv_in, wo_in,
    grad_out, loss_out,
    lat, feats, edges, target, wq, wk, wv, wo,
    kv, rim_out, rim_in, tpad, wof, won, query, kbd, vbd, attn, attn16, pred, got, back_out, back,
    gl, halo, plane_loss, deep_loss, mine,
    hello_two, hello_four, load_sem, rim_send, rim_recv, go_send, go_recv, ret_send, ret_recv,
    halo_send, halo_recv, pl_send, pl_recv, dl_send, dl_recv,
):
    me = lax.axis_index("ens")
    region = lax.axis_index("grid")
    wide, tall = regions // deep, members // CORES
    rx, rz = region // deep, lax.rem(region, deep)
    ry, rc = me // CORES, lax.rem(me, CORES)
    own_nodes, width = latent_in.shape
    points = feats_in.shape[0]
    variables = wo_in.shape[0]
    window = own_nodes + 2 * HALO
    head_size = width // HEADS
    heads = GROUP // head_size
    groups = width // GROUP
    lower = lax.rem(region + regions - 1, regions)
    upper = lax.rem(region + 1, regions)
    peers = [lax.rem(me + k, members) for k in range(members)]
    order = sorted(range(1, members), key=lambda k: -min(k // CORES, tall - k // CORES))
    plane, line = [], []
    def far(i, inner, outer):
        return -min(i // inner, outer - i // inner) - (min(i % inner, inner - i % inner) if inner > CORES else 0)

    for i in sorted(range(1, wide * tall), key=lambda i: far(i, tall, wide)):
        x, y = lax.rem(rx + i // tall, wide), lax.rem(ry + i % tall, tall)
        plane.append((i // tall, y * CORES + rc, x * deep + rz))
    for i in sorted(range(1, deep * CORES), key=lambda i: far(i, CORES, deep)):
        z, c = lax.rem(rz + i // CORES, deep), lax.rem(rc + i % CORES, CORES)
        line.append((i // CORES, ry * CORES + c, rx * deep + z))

    def load(src, dst, k):
        copy = pltpu.make_async_copy(src, dst, load_sem.at[k])
        copy.start()
        return copy

    def load_columns(src, dst, k):
        return [
            load(src.at[:, pl.ds(g * GROUP, GROUP)], dst.at[:, pl.ds(g * GROUP, GROUP)], k + g)
            for g in range(groups)
        ]

    has_lower, has_upper = region > 0, region < regions - 1
    other = ry * CORES + lax.rem(rc + 1, CORES)
    barrier = pltpu.get_barrier_semaphore()

    def signal(semaphore, member, r):
        pl.semaphore_signal(semaphore, inc=1, device_id=(member, r), device_id_type=MESH)

    def at_sides(below, above):
        pl.when(has_lower)(below)
        pl.when(has_upper)(above)

    def greet_side(r):
        signal(barrier, me, r)
        signal(barrier, other, r)

    at_sides(lambda: greet_side(lower), lambda: greet_side(upper))
    for k in order:
        signal(barrier, peers[k], region)
    for k in range(1, wide):
        signal(barrier, me, lax.rem(rx + k, wide) * deep + rz)

    load_lat = load(latent_in, lat, 0)
    load_wk = load_columns(wk_in, wk, 1)
    load_wv = load_columns(wv_in, wv, 5)
    load_feats = load(feats_in, feats, 9)
    load_wq = load_columns(wq_in, wq, 10)
    load_edges = load(edges_in, edges, 14)
    load_wo = load(wo_in, wo, 15)
    load_target = load(target_in, target, 16)

    def remote(src, dst, send_sem, recv_sem, member, r):
        return pltpu.make_async_remote_copy(
            src_ref=src, dst_ref=dst, send_sem=send_sem, recv_sem=recv_sem,
            device_id=(member, r), device_id_type=MESH,
        )

    def send(*what):
        copy = remote(*what)
        copy.start()
        return copy

    def swap(low_src, low_dst, up_src, up_dst, sems):
        down = remote(low_src, low_dst, sems[0].at[0], sems[1].at[0], me, lower)
        up = remote(up_src, up_dst, sems[0].at[1], sems[1].at[1], me, upper)
        at_sides(down.start, up.start)

        def below():
            down.wait_send()
            up.wait_recv()

        def above():
            up.wait_send()
            down.wait_recv()

        def finish():
            at_sides(below, above)

        return finish

    load_lat.wait()
    for g in range(groups):
        cols = pl.ds(g * GROUP, GROUP)
        for i, (loads, w) in enumerate(((load_wk, wk), (load_wv, wv))):
            loads[g].wait()
            kv[i, :, cols] = jnp.dot(lat[...], w[:, cols], preferred_element_type=F32)
    for side, row in enumerate((0, own_nodes - HALO)):
        rim_out[side] = jnp.concatenate(
            [kv[0, pl.ds(row, HALO), :], kv[1, pl.ds(row, HALO), :]], axis=0
        ).astype(BF16)
    @pl.when(jnp.logical_not(has_lower))
    def _():
        rim_in[0] = jnp.zeros(rim_in.shape[1:], BF16)
        halo[0] = jnp.zeros(halo.shape[1:], F32)

    @pl.when(jnp.logical_not(has_upper))
    def _():
        rim_in[1] = jnp.zeros(rim_in.shape[1:], BF16)
        halo[1] = jnp.zeros(halo.shape[1:], F32)

    sides = has_lower.astype(jnp.int32) + has_upper.astype(jnp.int32)
    pl.semaphore_wait(barrier, members - 1 + wide - 1 + CORES * sides)
    rims = swap(rim_out.at[0], rim_in.at[1], rim_out.at[1], rim_in.at[0], (rim_send, rim_recv))

    load_feats.wait()
    for g in range(groups):
        cols = pl.ds(g * GROUP, GROUP)
        load_wq[g].wait()
        query[:, cols] = jnp.dot(
            feats[...], wq[:, cols], preferred_element_type=F32
        ).astype(BF16)

    load_edges.wait()
    links = edges[...] - region * own_nodes
    links = jnp.where(links < 0, links + window, links)
    node = lax.broadcasted_iota(jnp.int32, (window, points), 0)
    node = jnp.where(node < own_nodes, node, jnp.where(node < own_nodes + HALO, node + HALO, node - HALO))
    count = jnp.zeros((window, points), F32)
    for e in range(edges_in.shape[0]):
        count = count + jnp.where(node == links[e : e + 1, :], 1.0, 0.0)
    linked = count > 0.0

    def head_of(rows):
        return lax.broadcasted_iota(jnp.int32, (rows, GROUP), 1) // head_size

    def spread(x, h):
        return jnp.where(head_of(x.shape[0]) == h, x, 0.0).astype(BF16)

    def gather(x):
        out = jnp.zeros((window, GROUP), F32)
        for h in range(heads):
            out = jnp.where(head_of(window) == h, x[h * window : (h + 1) * window], out)
        return out

    for g in range(groups):
        for h in range(heads):
            for i, dst in enumerate((kbd, vbd)):
                dst[g, pl.ds(h * window, own_nodes), :] = spread(kv[i, :, pl.ds(g * GROUP, GROUP)], h)

    load_target.wait()
    load_wo.wait()
    tpad[...] = jnp.zeros_like(tpad)
    tpad[pl.ds(0, variables), :] = target[...]
    wof[...] = jnp.zeros_like(wof)
    wof[pl.ds(0, variables), :] = wo[...].astype(F32)
    won[...] = wof[...].T.astype(BF16)
    pred[...] = jnp.zeros_like(pred)

    rims()
    def along(semaphore, z):
        for c in range(CORES):
            signal(semaphore, ry * CORES + c, rx * deep + z)

    pl.when(rz >= 2)(lambda: along(hello_two, rz - 2))
    pl.when(rz < deep - 2)(lambda: along(hello_two, rz + 2))
    for i, dst in enumerate((kbd, vbd)):
        for g in range(groups):
            cols = pl.ds(g * GROUP, GROUP)
            both = jnp.concatenate(
                [rim_in[side, :, cols].astype(F32)[i * HALO : (i + 1) * HALO] for side in range(2)], axis=0
            )
            for h in range(heads):
                dst[g, pl.ds(h * window + own_nodes, 2 * HALO), :] = spread(both, h)
    total = jnp.zeros((variables, points), F32)
    scale = head_size ** (-0.5)
    for g in range(groups):
        cols = pl.ds(g * GROUP, GROUP)
        scores = lax.dot_general(kbd[g], query[:, cols], NT, preferred_element_type=F32)
        parts = []
        for h in range(heads):
            s = jnp.where(linked, scores[h * window : (h + 1) * window], -jnp.inf)
            top = jnp.max(s, axis=0, keepdims=True)
            e = count * jnp.exp2((s - top) * (scale * LOG2E))
            a = e * (1.0 / jnp.sum(e, axis=0, keepdims=True))
            attn[g, pl.ds(h * window, window), :] = a
            parts.append(a.astype(BF16))
        a16 = jnp.concatenate(parts, axis=0)
        attn16[g] = a16
        ctx = lax.dot_general(vbd[g], a16, TN, preferred_element_type=F32).astype(BF16)
        total = total + jnp.dot(wo[:, cols], ctx, preferred_element_type=F32)
    pred[pl.ds(0, variables), :] = total

    gone = [
        send(pred.at[pl.ds(pl.multiple_of(peers[k] * ROWS, ROWS), ROWS)], got.at[k],
             go_send.at[k], go_recv.at[k], peers[k], region)
        for k in order
    ]
    first = pl.multiple_of(me * ROWS, ROWS)
    got[0] = pred[pl.ds(first, ROWS), :]
    for copy in gone:
        copy.wait()
    pl.semaphore_wait(hello_two, CORES * ((rz >= 2).astype(jnp.int32) + (rz < deep - 2).astype(jnp.int32)))
    along(hello_four, lax.rem(rz + 4, deep))

    coeff = 1.0 - (1.0 - ALPHA) / members
    pair = coeff / (members * (members - 1))
    loss_part = jnp.zeros((8, 128), F32)
    for top in range(0, ROWS, 8):
        row = lax.broadcasted_iota(jnp.int32, (8, 128), 0) + first + top
        valid = row < variables
        block_loss = jnp.zeros((8, 128), F32)
        for left in range(0, points, 128):
            at = (pl.ds(top, 8), pl.ds(left, 128))
            goal = tpad[pl.ds(first + top, 8), pl.ds(left, 128)]
            ps = [got[(k,) + at] for k in range(members)]
            slopes = [None] * members
            near = jnp.zeros((8, 128), F32)
            apart = jnp.full((8, 128), 0.5 * members * math.sqrt(DELTA_SQ), F32)
            grads = []
            for i in range(members):
                d = ps[i] - goal
                sq = d * d + DELTA_SQ
                inv = lax.rsqrt(sq)
                near = near + sq * inv
                grads.append(d * inv)
            for i in range(members):
                for j in range(i + 1, members):
                    d = ps[i] - ps[j]
                    sq = d * d + DELTA_SQ
                    inv = lax.rsqrt(sq)
                    apart = apart + sq * inv
                    d = d * inv
                    slopes[i] = d if slopes[i] is None else slopes[i] + d
                    slopes[j] = -d if slopes[j] is None else slopes[j] - d
            block_loss = block_loss + (near * (1.0 / members) - apart * pair)
            for i in range(members):
                back_out[(i,) + at] = (grads[i] * (1.0 / members) - slopes[i] * pair).astype(BF16)
        loss_part = loss_part + jnp.where(valid, block_loss, 0.0)

    returned = []
    for k in order:
        owner = lax.rem(me + members - k, members)
        returned.append(
            send(back_out.at[k], back.at[pl.ds(first, ROWS)],
                 ret_send.at[k], ret_recv.at[k], owner, region)
        )
    loss_part = jnp.sum(loss_part, axis=0, keepdims=True)
    mine[0] = loss_part
    slot = rx * tall + ry
    plane_loss[slot] = loss_part
    plane_sent = [
        send(mine.at[0], plane_loss.at[slot], pl_send.at[k], pl_recv.at[k], m, r)
        for k, (_, m, r) in enumerate(plane)
    ]
    back[pl.ds(first, ROWS), :] = back_out[0]

    for copy in returned:
        copy.wait()
    gk, gv = [], []
    for g in range(groups):
        cols = pl.ds(g * GROUP, GROUP)
        gc = jnp.dot(won[cols, :], back[...], preferred_element_type=F32).astype(BF16)
        ga = jnp.dot(vbd[g], gc, preferred_element_type=F32)
        parts = []
        for h in range(heads):
            a = attn[g, pl.ds(h * window, window), :]
            t = a * ga[h * window : (h + 1) * window]
            parts.append(t - a * jnp.sum(t, axis=0, keepdims=True))
        gs = jnp.concatenate(parts, axis=0).astype(BF16)
        gk.append((gather(jnp.dot(gs, query[:, cols], preferred_element_type=F32)) * scale).astype(BF16))
        gv.append(gather(lax.dot_general(attn16[g], gc, NT, preferred_element_type=F32)).astype(BF16))
    gk = jnp.concatenate(gk, axis=1)
    gv = jnp.concatenate(gv, axis=1)

    for copy in plane_sent:
        copy.wait()
    pl.semaphore_wait(hello_four, CORES)
    loss_part = plane_loss[0]
    for k in range(1, wide * tall):
        loss_part = loss_part + plane_loss[k]
    loss_part = jnp.broadcast_to(jnp.sum(loss_part, axis=1, keepdims=True) * (1.0 / npts), loss_part.shape)
    mine[1] = loss_part
    slot = rz * CORES + rc
    deep_loss[slot] = loss_part
    line_sent = [
        send(mine.at[1], deep_loss.at[slot], dl_send.at[k], dl_recv.at[k], m, r)
        for k, (_, m, r) in enumerate(line)
    ]

    for c in range(width // GROUP):
        cols = pl.ds(c * GROUP, GROUP)
        out = lax.dot_general(gk, wk[cols, :], NT, preferred_element_type=F32)
        out = out + lax.dot_general(gv, wv[cols, :], NT, preferred_element_type=F32)
        gl[:, cols] = out[own_nodes:]
        grad_out[:, cols] = out[:own_nodes]
    rims = swap(
        gl.at[pl.ds(0, HALO)], halo.at[1], gl.at[pl.ds(HALO, HALO)], halo.at[0],
        (halo_send, halo_recv),
    )
    rims()
    grad_out[pl.ds(0, HALO), :] += halo[0]
    grad_out[pl.ds(own_nodes - HALO, HALO), :] += halo[1]

    for copy in line_sent:
        copy.wait()
    loss_part = deep_loss[0]
    for k in range(1, deep * CORES):
        loss_part = loss_part + deep_loss[k]
    loss_out[...] = jnp.broadcast_to(loss_part, loss_out.shape)


def finish(grad, loss, grad_out, loss_out, one, sem):
    copies = [pltpu.make_async_copy(grad, grad_out, sem.at[0]), pltpu.make_async_copy(one, loss_out, sem.at[1])]
    copies[0].start()
    one[...] = loss[pl.ds(0, 1), pl.ds(0, 1)]
    copies[1].start()
    for copy in copies:
        copy.wait()


def local(members, regions, mesh_latent, grid_feat, edges, target, w_query, w_key, w_value, w_out):
    latent = mesh_latent[0]
    feats = grid_feat[0]
    own_nodes, width = latent.shape
    points, links = edges.shape
    variables = target.shape[1]
    window = own_nodes + 2 * HALO
    deep = math.gcd(regions, 8) if regions > 8 else 2
    wide, tall = regions // deep, members // CORES
    groups = width // GROUP
    stack = window * GROUP // (width // HEADS)
    padded = members * ROWS
    dma = pltpu.SemaphoreType.DMA
    any_space = pl.BlockSpec(memory_space=pltpu.HBM)
    vmem = pl.BlockSpec(memory_space=pltpu.VMEM)
    grad, loss = pl.pallas_call(
        functools.partial(kernel, members, regions, deep, points * regions * variables),
        out_shape=(
            jax.ShapeDtypeStruct((own_nodes, width), F32),
            jax.ShapeDtypeStruct((8, 128), F32),
        ),
        in_specs=[any_space] * 8,
        out_specs=(vmem, vmem),
        scratch_shapes=[
            pltpu.VMEM((own_nodes, width), BF16),
            pltpu.VMEM((points, width), BF16),
            pltpu.VMEM((links, points), jnp.int32),
            pltpu.VMEM((variables, points), F32),
            pltpu.VMEM((width, width), BF16),
            pltpu.VMEM((width, width), BF16),
            pltpu.VMEM((width, width), BF16),
            pltpu.VMEM((variables, width), BF16),
            pltpu.VMEM((2, own_nodes, width), F32),
            pltpu.VMEM((2, 2 * HALO, width), BF16),
            pltpu.VMEM((2, 2 * HALO, width), BF16),
            pltpu.VMEM((padded, points), F32),
            pltpu.VMEM((padded, width), F32),
            pltpu.VMEM((width, padded), BF16),
            pltpu.VMEM((points, width), BF16),
            pltpu.VMEM((groups, stack, GROUP), BF16),
            pltpu.VMEM((groups, stack, GROUP), BF16),
            pltpu.VMEM((groups, stack, points), F32),
            pltpu.VMEM((groups, stack, points), BF16),
            pltpu.VMEM((padded, points), F32),
            pltpu.VMEM((members, ROWS, points), F32),
            pltpu.VMEM((members, ROWS, points), BF16),
            pltpu.VMEM((padded, points), BF16),
            pltpu.VMEM((2 * HALO, width), F32),
            pltpu.VMEM((2, HALO, width), F32),
            pltpu.VMEM((wide * tall, 1, 128), F32),
            pltpu.VMEM((deep * CORES, 1, 128), F32),
            pltpu.VMEM((2, 1, 128), F32),
            pltpu.SemaphoreType.REGULAR,
            pltpu.SemaphoreType.REGULAR,
            dma((17,)),
            dma((2,)), dma((2,)),
            dma((members,)), dma((members,)),
            dma((members,)), dma((members,)),
            dma((2,)), dma((2,)),
            dma((wide * tall,)), dma((wide * tall,)),
            dma((deep * CORES,)), dma((deep * CORES,)),
        ],
        compiler_params=pltpu.CompilerParams(
            collective_id=0, has_side_effects=True, vmem_limit_bytes=24 * 1024 * 1024
        ),
    )(*[pltpu.with_memory_space_constraint(x, pltpu.HBM) for x in (latent, feats, edges.T, target.T, w_query, w_key, w_value, w_out.T)])
    grad, loss = pl.pallas_call(
        finish,
        out_shape=(
            jax.ShapeDtypeStruct((own_nodes, width), F32),
            jax.ShapeDtypeStruct((1, 1), F32),
        ),
        in_specs=[vmem, vmem],
        out_specs=(pl.BlockSpec(memory_space=pltpu.HBM), pl.BlockSpec(memory_space=pltpu.HBM)),
        scratch_shapes=[pltpu.VMEM((1, 1), F32), dma((2,))],
        compiler_params=pltpu.CompilerParams(vmem_limit_bytes=4 * 1024 * 1024),
    )(grad, loss)
    return grad[None], loss[0, 0]


def solution(mesh):
    in_specs = (
        P("ens", "grid", None),
        P("ens", "grid", None),
        P("grid", None),
        P("grid", None),
        P(),
        P(),
        P(),
        P(),
    )
    out_specs = (P("ens", "grid", None), P())
    return jax.shard_map(
        functools.partial(local, mesh.shape["ens"], mesh.shape["grid"]),
        mesh=mesh, in_specs=in_specs, out_specs=out_specs, check_vma=False,
    )
```

```python
import functools
import math

import jax
import jax.numpy as jnp
from jax import lax
from jax.experimental import pallas as pl
from jax.experimental.pallas import tpu as pltpu
from jax.sharding import PartitionSpec as P

HEADS = 16
HALO = 8
DELTA_SQ = 0.01
ALPHA = 0.95
LOG2E = math.log2(math.e)

MESH = pl.DeviceIdType.MESH
F32 = jnp.float32
BF16 = jnp.bfloat16

CORES = 2
ROWS = 16
GROUP = 256
NT = (((1,), (1,)), ((), ()))
TN = (((0,), (0,)), ((), ()))


def kernel(
    members, regions, deep, npts,
    latent_in, feats_in, edges_in, target_in, wq_in, wk_in, wv_in, wo_in,
    grad_out, loss_out,
    lat, feats, edges, target, wq, wk, wv, wo,
    kv, rim_out, rim_in, tpad, wof, won, query, scores, vt, vbd, attn, attn16, pred, got, back_out, back,
    gl, halo, plane_loss, deep_loss, mine,
    hello_one, hello_two, hello_four, load_sem, rim_send, rim_recv, go_send, go_recv, ret_send, ret_recv,
    halo_send, halo_recv, pl_send, pl_recv, dl_send, dl_recv,
):
    me = lax.axis_index("ens")
    region = lax.axis_index("grid")
    wide, tall = regions // deep, members // CORES
    rx, rz = region // deep, lax.rem(region, deep)
    ry, rc = me // CORES, lax.rem(me, CORES)
    own_nodes, width = latent_in.shape
    points = feats_in.shape[0]
    variables = wo_in.shape[0]
    window = own_nodes + 2 * HALO
    head_size = width // HEADS
    heads = GROUP // head_size
    groups = width // GROUP
    lower = lax.rem(region + regions - 1, regions)
    upper = lax.rem(region + 1, regions)
    peers = [lax.rem(me + k, members) for k in range(members)]
    order = sorted(range(1, members), key=lambda k: -min(k // CORES, tall - k // CORES))
    plane, line = [], []
    def far(i, inner, outer):
        return -min(i // inner, outer - i // inner) - (min(i % inner, inner - i % inner) if inner > CORES else 0)

    for i in sorted(range(1, wide * tall), key=lambda i: far(i, tall, wide)):
        x, y = lax.rem(rx + i // tall, wide), lax.rem(ry + i % tall, tall)
        plane.append((i // tall, y * CORES + rc, x * deep + rz))
    for i in sorted(range(1, deep * CORES), key=lambda i: far(i, CORES, deep)):
        z, c = lax.rem(rz + i // CORES, deep), lax.rem(rc + i % CORES, CORES)
        line.append((i // CORES, ry * CORES + c, rx * deep + z))

    def load(src, dst, k):
        copy = pltpu.make_async_copy(src, dst, load_sem.at[k])
        copy.start()
        return copy

    def load_columns(src, dst, k):
        return [
            load(src.at[:, pl.ds(g * GROUP, GROUP)], dst.at[:, pl.ds(g * GROUP, GROUP)], k + g)
            for g in range(groups)
        ]

    has_lower, has_upper = region > 0, region < regions - 1
    other = ry * CORES + lax.rem(rc + 1, CORES)
    barrier = pltpu.get_barrier_semaphore()

    def signal(semaphore, member, r):
        pl.semaphore_signal(semaphore, inc=1, device_id=(member, r), device_id_type=MESH)

    def at_sides(below, above):
        pl.when(has_lower)(below)
        pl.when(has_upper)(above)

    def greet_side(r):
        signal(barrier, me, r)
        signal(barrier, other, r)

    at_sides(lambda: greet_side(lower), lambda: greet_side(upper))
    steps_y = [lax.rem(ry + step, tall) for step in (1, tall - 1)]
    next_x = [lax.rem(rx + step, wide) * deep + rz for step in (1, wide - 1)]
    for y in steps_y:
        for c in range(CORES):
            signal(barrier, y * CORES + c, region)
    for r in next_x:
        signal(barrier, me, r)
    signal(barrier, other, region)

    load_lat = load(latent_in, lat, 0)
    load_wk = load_columns(wk_in, wk, 1)
    load_wv = load_columns(wv_in, wv, 5)

    def remote(src, dst, send_sem, recv_sem, member, r):
        return pltpu.make_async_remote_copy(
            src_ref=src, dst_ref=dst, send_sem=send_sem, recv_sem=recv_sem,
            device_id=(member, r), device_id_type=MESH,
        )

    def send(*what):
        copy = remote(*what)
        copy.start()
        return copy

    def drain(bytes_of, semaphore):
        pltpu.make_async_copy(bytes_of, bytes_of, semaphore).wait()

    def swap(low_src, low_dst, up_src, up_dst, sems, k=0):
        down = remote(low_src, low_dst, sems[0].at[k], sems[1].at[k], me, lower)
        up = remote(up_src, up_dst, sems[0].at[k + 1], sems[1].at[k + 1], me, upper)
        at_sides(down.start, up.start)

        def below():
            down.wait_send()
            up.wait_recv()

        def above():
            up.wait_send()
            down.wait_recv()

        def finish():
            at_sides(below, above)

        return finish

    load_lat.wait()
    for g in range(groups):
        cols = pl.ds(g * GROUP, GROUP)
        for i, (loads, w) in enumerate(((load_wk, wk), (load_wv, wv))):
            loads[g].wait()
            if g == groups - 1 and i == 0:
                load_feats = load(feats_in, feats, 9)
                load_wq = load_columns(wq_in, wq, 10)
                load_edges = load(edges_in, edges, 14)
                load_wo = load(wo_in, wo, 15)
                load_target = load(target_in, target, 16)
            kv[i, :, cols] = jnp.dot(lat[...], w[:, cols], preferred_element_type=F32)
    for side, row in enumerate((0, own_nodes - HALO)):
        rim_out[side] = jnp.concatenate(
            [kv[0, pl.ds(row, HALO), :], kv[1, pl.ds(row, HALO), :]], axis=0
        ).astype(BF16)
    @pl.when(jnp.logical_not(has_lower))
    def _():
        rim_in[0] = jnp.zeros(rim_in.shape[1:], BF16)
        halo[0] = jnp.zeros(halo.shape[1:], F32)

    @pl.when(jnp.logical_not(has_upper))
    def _():
        rim_in[1] = jnp.zeros(rim_in.shape[1:], BF16)
        halo[1] = jnp.zeros(halo.shape[1:], F32)

    sides = has_lower.astype(jnp.int32) + has_upper.astype(jnp.int32)
    pl.semaphore_wait(barrier, 2 * CORES + 2 + 1 + CORES * sides)
    rims = swap(rim_out.at[0], rim_in.at[1], rim_out.at[1], rim_in.at[0], (rim_send, rim_recv))

    for y in steps_y:
        signal(hello_one, y * CORES + rc, region)
    for r in next_x:
        signal(hello_one, me, r)

    load_feats.wait()
    for g in range(groups):
        cols = pl.ds(g * GROUP, GROUP)
        load_wq[g].wait()
        query[:, cols] = jnp.dot(
            feats[...], wq[:, cols], preferred_element_type=F32
        ).astype(BF16)

    load_edges.wait()
    links = edges[...] - region * own_nodes
    links = jnp.where(links < 0, links + window, links)
    node = lax.broadcasted_iota(jnp.int32, (window, points), 0)
    node = jnp.where(node < own_nodes, node, jnp.where(node < own_nodes + HALO, node + HALO, node - HALO))
    count = jnp.zeros((window, points), F32)
    for e in range(edges_in.shape[0]):
        count = count + jnp.where(node == links[e : e + 1, :], 1.0, 0.0)
    linked = count > 0.0

    def head_of(rows):
        return lax.broadcasted_iota(jnp.int32, (rows, GROUP), 1) // head_size

    def spread(x, h):
        return jnp.where(head_of(x.shape[0]) == h, x, 0.0).astype(BF16)

    def gather(x):
        own, rim = x[:own_nodes], x[heads * own_nodes : heads * own_nodes + 2 * HALO]
        for h in range(1, heads):
            at = heads * own_nodes + h * 2 * HALO
            own = jnp.where(head_of(own_nodes) == h, x[h * own_nodes : (h + 1) * own_nodes], own)
            rim = jnp.where(head_of(2 * HALO) == h, x[at : at + 2 * HALO], rim)
        return jnp.concatenate([own, rim], axis=0)

    def fold(op, reduce, own, rim):
        pieces = [x[i : i + 8] for x in (own, rim) for i in range(0, x.shape[0], 8)]
        while len(pieces) > 1:
            pieces = [op(*pair) for pair in zip(pieces[::2], pieces[1::2])] + pieces[len(pieces) // 2 * 2 :]
        return reduce(pieces[0], axis=0, keepdims=True)

    stacked = heads * own_nodes
    for g in range(groups):
        cols = pl.ds(g * GROUP, GROUP)
        kb = jnp.concatenate([spread(kv[0, :, cols], h) for h in range(heads)], axis=0)
        vb = jnp.concatenate([spread(kv[1, :, cols], h) for h in range(heads)], axis=0)
        vbd[g, pl.ds(0, stacked), :] = vb
        vt[g, :, pl.ds(0, stacked)] = vb.T
        own = lax.dot_general(kb, query[:, cols], NT, preferred_element_type=F32)
        for h in range(heads):
            rows = slice(h * own_nodes, (h + 1) * own_nodes)
            scores[g, rows, :] = jnp.where(linked[:own_nodes], own[rows], -jnp.inf)

    load_target.wait()
    load_wo.wait()
    tpad[...] = jnp.zeros_like(tpad)
    tpad[pl.ds(0, variables), :] = target[...]
    wof[...] = jnp.zeros_like(wof)
    wof[pl.ds(0, variables), :] = wo[...].astype(F32)
    won[...] = wof[...].T.astype(BF16)
    pred[...] = jnp.zeros_like(pred)

    rims()
    def along(semaphore, z):
        for c in range(CORES):
            signal(semaphore, ry * CORES + c, rx * deep + z)

    pl.when(rz >= 2)(lambda: along(hello_two, rz - 2))
    pl.when(rz < deep - 2)(lambda: along(hello_two, rz + 2))
    rim_scores = []
    for g in range(groups):
        cols = pl.ds(g * GROUP, GROUP)
        both = [
            jnp.concatenate(
                [rim_in[side, :, cols].astype(F32)[i * HALO : (i + 1) * HALO] for side in range(2)], axis=0
            )
            for i in range(2)
        ]
        kb = jnp.concatenate([spread(both[0], h) for h in range(heads)], axis=0)
        vb = jnp.concatenate([spread(both[1], h) for h in range(heads)], axis=0)
        rim_scores.append(lax.dot_general(kb, query[:, cols], NT, preferred_element_type=F32))
        vbd[g, pl.ds(stacked, heads * 2 * HALO), :] = vb
        vt[g, :, pl.ds(stacked, heads * 2 * HALO)] = vb.T
    total = jnp.zeros((variables, points), F32)
    scale = head_size ** (-0.5)
    for g in range(groups):
        cols = pl.ds(g * GROUP, GROUP)
        parts, rim_parts = [], []
        for h in range(heads):
            rows = pl.ds(h * own_nodes, own_nodes)
            s = scores[g, rows, :]
            r = jnp.where(linked[own_nodes:], rim_scores[g][h * 2 * HALO : (h + 1) * 2 * HALO], -jnp.inf)
            top = fold(jnp.maximum, jnp.max, s, r)
            e = count[:own_nodes] * jnp.exp2((s - top) * (scale * LOG2E))
            f = count[own_nodes:] * jnp.exp2((r - top) * (scale * LOG2E))
            inv = 1.0 / fold(jnp.add, jnp.sum, e, f)
            e, f = e * inv, f * inv
            attn[g, rows, :] = e
            attn[g, pl.ds(stacked + h * 2 * HALO, 2 * HALO), :] = f
            parts.append(e.astype(BF16))
            rim_parts.append(f.astype(BF16))
        a16 = jnp.concatenate(parts + rim_parts, axis=0)
        attn16[g] = a16
        ctx = jnp.dot(vt[g], a16, preferred_element_type=F32).astype(BF16)
        total = total + jnp.dot(wo[:, cols], ctx, preferred_element_type=F32)
    pred[pl.ds(0, variables), :] = total

    pl.semaphore_wait(hello_one, 4)
    for k in order:
        send(pred.at[pl.ds(pl.multiple_of(peers[k] * ROWS, ROWS), ROWS)], got.at[k],
             go_send, go_recv, peers[k], region)
    first = pl.multiple_of(me * ROWS, ROWS)
    got[0] = pred[pl.ds(first, ROWS), :]
    drain(got.at[pl.ds(1, members - 1)], go_send)
    drain(got.at[pl.ds(1, members - 1)], go_recv)
    pl.semaphore_wait(hello_two, CORES * ((rz >= 2).astype(jnp.int32) + (rz < deep - 2).astype(jnp.int32)))
    along(hello_four, lax.rem(rz + 4, deep))

    coeff = 1.0 - (1.0 - ALPHA) / members
    pair = coeff / (members * (members - 1))
    loss_part = jnp.zeros((8, 128), F32)
    for top in range(0, ROWS, 8):
        row = lax.broadcasted_iota(jnp.int32, (8, 128), 0) + first + top
        valid = row < variables
        block_loss = jnp.zeros((8, 128), F32)
        for left in range(0, points, 128):
            at = (pl.ds(top, 8), pl.ds(left, 128))
            goal = tpad[pl.ds(first + top, 8), pl.ds(left, 128)]
            ps = [got[(k,) + at] for k in range(members)]
            slopes = [None] * members
            near = jnp.zeros((8, 128), F32)
            apart = jnp.full((8, 128), 0.5 * members * math.sqrt(DELTA_SQ), F32)
            grads = []
            for i in range(members):
                d = ps[i] - goal
                sq = d * d + DELTA_SQ
                inv = lax.rsqrt(sq)
                near = near + sq * inv
                grads.append(d * inv)
            for i in range(members):
                for j in range(i + 1, members):
                    d = ps[i] - ps[j]
                    sq = d * d + DELTA_SQ
                    inv = lax.rsqrt(sq)
                    apart = apart + sq * inv
                    d = d * inv
                    slopes[i] = d if slopes[i] is None else slopes[i] + d
                    slopes[j] = -d if slopes[j] is None else slopes[j] - d
            block_loss = block_loss + (near * (1.0 / members) - apart * pair)
            for i in range(members):
                back_out[(i,) + at] = (grads[i] * (1.0 / members) - slopes[i] * pair).astype(BF16)
        loss_part = loss_part + jnp.where(valid, block_loss, 0.0)

    for k in order:
        owner = lax.rem(me + members - k, members)
        send(back_out.at[k], back.at[pl.ds(first, ROWS)], ret_send, ret_recv, owner, region)
    loss_part = jnp.sum(loss_part, axis=0, keepdims=True)
    mine[0] = loss_part
    slot = rx * tall + ry
    plane_loss[slot] = loss_part
    for _, m, r in plane:
        send(mine.at[0], plane_loss.at[slot], pl_send, pl_recv, m, r)
    back[pl.ds(first, ROWS), :] = back_out[0]

    drain(back_out.at[pl.ds(1, members - 1)], ret_send)
    drain(back_out.at[pl.ds(1, members - 1)], ret_recv)
    gcs, gas, gk, gv = [], [], [], []
    for g in range(groups):
        gc = jnp.dot(won[pl.ds(g * GROUP, GROUP), :], back[...], preferred_element_type=F32).astype(BF16)
        gcs.append(gc)
    for g in range(groups):
        gas.append(jnp.dot(vbd[g], gcs[g], preferred_element_type=F32))
    for g in range(groups):
        gv.append(gather(lax.dot_general(attn16[g], gcs[g], NT, preferred_element_type=F32)).astype(BF16))
    for g in range(groups):
        cols = pl.ds(g * GROUP, GROUP)
        ga = gas[g]
        parts, rim_parts = [], []
        for h in range(heads):
            at = stacked + h * 2 * HALO
            a, f = attn[g, pl.ds(h * own_nodes, own_nodes), :], attn[g, pl.ds(at, 2 * HALO), :]
            t, u = a * ga[h * own_nodes : (h + 1) * own_nodes], f * ga[at : at + 2 * HALO]
            mean = fold(jnp.add, jnp.sum, t, u)
            parts.append(t - a * mean)
            rim_parts.append(u - f * mean)
        gs = jnp.concatenate(parts + rim_parts, axis=0).astype(BF16)
        gk.append((gather(jnp.dot(gs, query[:, cols], preferred_element_type=F32)) * scale).astype(BF16))
    gk = jnp.concatenate(gk, axis=1)
    gv = jnp.concatenate(gv, axis=1)

    drain(plane_loss.at[pl.ds(1, len(plane))], pl_send)
    drain(plane_loss.at[pl.ds(1, len(plane))], pl_recv)
    pl.semaphore_wait(hello_four, CORES)
    loss_part = plane_loss[0]
    for k in range(1, wide * tall):
        loss_part = loss_part + plane_loss[k]
    loss_part = jnp.broadcast_to(jnp.sum(loss_part, axis=1, keepdims=True) * (1.0 / npts), loss_part.shape)
    mine[1] = loss_part
    slot = rz * CORES + rc
    deep_loss[slot] = loss_part
    for _, m, r in line:
        send(mine.at[1], deep_loss.at[slot], dl_send, dl_recv, m, r)

    rims = []
    for c in range(width // GROUP):
        cols = pl.ds(c * GROUP, GROUP)
        out = lax.dot_general(gk, wk[cols, :], NT, preferred_element_type=F32)
        out = out + lax.dot_general(gv, wv[cols, :], NT, preferred_element_type=F32)
        gl[:, cols] = out[own_nodes:]
        grad_out[:, cols] = out[:own_nodes]
        if c % 2:
            half = pl.ds((c - 1) * GROUP, 2 * GROUP)
            rims.append(swap(
                gl.at[pl.ds(0, HALO), half], halo.at[1, :, half],
                gl.at[pl.ds(HALO, HALO), half], halo.at[0, :, half], (halo_send, halo_recv), c - 1,
            ))
    for finish_rims in rims:
        finish_rims()
    grad_out[pl.ds(0, HALO), :] += halo[0]
    grad_out[pl.ds(own_nodes - HALO, HALO), :] += halo[1]

    drain(deep_loss.at[pl.ds(1, len(line))], dl_send)
    drain(deep_loss.at[pl.ds(1, len(line))], dl_recv)
    loss_part = deep_loss[0]
    for k in range(1, deep * CORES):
        loss_part = loss_part + deep_loss[k]
    loss_out[...] = jnp.broadcast_to(loss_part, loss_out.shape)


def finish(grad, loss, grad_out, loss_out, one, sem):
    copies = [pltpu.make_async_copy(grad, grad_out, sem.at[0]), pltpu.make_async_copy(one, loss_out, sem.at[1])]
    copies[0].start()
    one[...] = loss[pl.ds(0, 1), pl.ds(0, 1)]
    copies[1].start()
    for copy in copies:
        copy.wait()


def local(members, regions, mesh_latent, grid_feat, edges, target, w_query, w_key, w_value, w_out):
    latent = mesh_latent[0]
    feats = grid_feat[0]
    own_nodes, width = latent.shape
    points, links = edges.shape
    variables = target.shape[1]
    window = own_nodes + 2 * HALO
    deep = math.gcd(regions, 8) if regions > 8 else 2
    wide, tall = regions // deep, members // CORES
    groups = width // GROUP
    stack = window * GROUP // (width // HEADS)
    padded = members * ROWS
    dma = pltpu.SemaphoreType.DMA
    any_space = pl.BlockSpec(memory_space=pltpu.HBM)
    vmem = pl.BlockSpec(memory_space=pltpu.VMEM)
    grad, loss = pl.pallas_call(
        functools.partial(kernel, members, regions, deep, points * regions * variables),
        out_shape=(
            jax.ShapeDtypeStruct((own_nodes, width), F32),
            jax.ShapeDtypeStruct((8, 128), F32),
        ),
        in_specs=[any_space] * 8,
        out_specs=(vmem, vmem),
        scratch_shapes=[
            pltpu.VMEM((own_nodes, width), BF16),
            pltpu.VMEM((points, width), BF16),
            pltpu.VMEM((links, points), jnp.int32),
            pltpu.VMEM((variables, points), F32),
            pltpu.VMEM((width, width), BF16),
            pltpu.VMEM((width, width), BF16),
            pltpu.VMEM((width, width), BF16),
            pltpu.VMEM((variables, width), BF16),
            pltpu.VMEM((2, own_nodes, width), F32),
            pltpu.VMEM((2, 2 * HALO, width), BF16),
            pltpu.VMEM((2, 2 * HALO, width), BF16),
            pltpu.VMEM((padded, points), F32),
            pltpu.VMEM((padded, width), F32),
            pltpu.VMEM((width, padded), BF16),
            pltpu.VMEM((points, width), BF16),
            pltpu.VMEM((groups, stack, points), F32),
            pltpu.VMEM((groups, GROUP, stack), BF16),
            pltpu.VMEM((groups, stack, GROUP), BF16),
            pltpu.VMEM((groups, stack, points), F32),
            pltpu.VMEM((groups, stack, points), BF16),
            pltpu.VMEM((padded, points), F32),
            pltpu.VMEM((members, ROWS, points), F32),
            pltpu.VMEM((members, ROWS, points), BF16),
            pltpu.VMEM((padded, points), BF16),
            pltpu.VMEM((2 * HALO, width), F32),
            pltpu.VMEM((2, HALO, width), F32),
            pltpu.VMEM((wide * tall, 1, 128), F32),
            pltpu.VMEM((deep * CORES, 1, 128), F32),
            pltpu.VMEM((2, 1, 128), F32),
            pltpu.SemaphoreType.REGULAR,
            pltpu.SemaphoreType.REGULAR,
            pltpu.SemaphoreType.REGULAR,
            dma((17,)),
            dma((2,)), dma((2,)),
            dma, dma,
            dma, dma,
            dma((4,)), dma((4,)),
            dma, dma,
            dma, dma,
        ],
        compiler_params=pltpu.CompilerParams(
            collective_id=0, has_side_effects=True, vmem_limit_bytes=24 * 1024 * 1024
        ),
    )(*[pltpu.with_memory_space_constraint(x, pltpu.HBM) for x in (latent, feats, edges.T, target.T, w_query, w_key, w_value, w_out.T)])
    grad, loss = pl.pallas_call(
        finish,
        out_shape=(
            jax.ShapeDtypeStruct((own_nodes, width), F32),
            jax.ShapeDtypeStruct((1, 1), F32),
        ),
        in_specs=[vmem, vmem],
        out_specs=(pl.BlockSpec(memory_space=pltpu.HBM), pl.BlockSpec(memory_space=pltpu.HBM)),
        scratch_shapes=[pltpu.VMEM((1, 1), F32), dma((2,))],
        compiler_params=pltpu.CompilerParams(vmem_limit_bytes=4 * 1024 * 1024),
    )(grad, loss)
    return grad[None], loss[0, 0]


def solution(mesh):
    in_specs = (
        P("ens", "grid", None),
        P("ens", "grid", None),
        P("grid", None),
        P("grid", None),
        P(),
        P(),
        P(),
        P(),
    )
    out_specs = (P("ens", "grid", None), P())
    return jax.shard_map(
        functools.partial(local, mesh.shape["ens"], mesh.shape["grid"]),
        mesh=mesh, in_specs=in_specs, out_specs=out_specs, check_vma=False,
    )
```

```python
import functools
import math

import jax
import jax.numpy as jnp
from jax import lax
from jax.experimental import pallas as pl
from jax.experimental.pallas import tpu as pltpu
from jax.sharding import PartitionSpec as P

HEADS = 16
HALO = 8
DELTA_SQ = 0.01
ALPHA = 0.95
LOG2E = math.log2(math.e)

MESH = pl.DeviceIdType.MESH
F32 = jnp.float32
BF16 = jnp.bfloat16

CORES = 2
ROWS = 16
GROUP = 256
NT = (((1,), (1,)), ((), ()))
TN = (((0,), (0,)), ((), ()))


def kernel(
    members, regions, deep, npts,
    latent_in, feats_in, edges_in, target_in, wq_in, wk_in, wv_in, wo_in,
    grad_out, loss_out,
    lat, feats, edges, target, wq, wk, wv, wo,
    kv, rim_out, rim_in, tpad, wof, won, query, scores, vt, vbd, attn, attn16, pred, got, back_out, back,
    gl, halo, plane_loss, deep_loss, mine,
    hello_one, hello_two, hello_four, load_sem, rim_send, rim_recv, go_send, go_recv, ret_send, ret_recv,
    halo_send, halo_recv, pl_send, pl_recv, dl_send, dl_recv,
):
    me = lax.axis_index("ens")
    region = lax.axis_index("grid")
    wide, tall = regions // deep, members // CORES
    rx, rz = region // deep, lax.rem(region, deep)
    ry, rc = me // CORES, lax.rem(me, CORES)
    own_nodes, width = latent_in.shape
    points = feats_in.shape[0]
    variables = wo_in.shape[0]
    window = own_nodes + 2 * HALO
    head_size = width // HEADS
    heads = GROUP // head_size
    groups = width // GROUP
    lower = lax.rem(region + regions - 1, regions)
    upper = lax.rem(region + 1, regions)
    peers = [lax.rem(me + k, members) for k in range(members)]
    order = sorted(range(1, members), key=lambda k: -min(k // CORES, tall - k // CORES))
    plane, line = [], []
    def far(i, inner, outer):
        return -min(i // inner, outer - i // inner) - (min(i % inner, inner - i % inner) if inner > CORES else 0)

    for i in sorted(range(1, wide * tall), key=lambda i: far(i, tall, wide)):
        x, y = lax.rem(rx + i // tall, wide), lax.rem(ry + i % tall, tall)
        plane.append((i // tall, y * CORES + rc, x * deep + rz))
    for i in sorted(range(1, deep * CORES), key=lambda i: far(i, CORES, deep)):
        z, c = lax.rem(rz + i // CORES, deep), lax.rem(rc + i % CORES, CORES)
        line.append((i // CORES, ry * CORES + c, rx * deep + z))

    def load(src, dst, k):
        copy = pltpu.make_async_copy(src, dst, load_sem.at[k])
        copy.start()
        return copy

    def load_columns(src, dst, k):
        half = width // 2
        return [
            load(src.at[:, pl.ds(i * half, half)], dst.at[:, pl.ds(i * half, half)], k + i) for i in range(2)
        ]

    has_lower, has_upper = region > 0, region < regions - 1
    other = ry * CORES + lax.rem(rc + 1, CORES)
    barrier = pltpu.get_barrier_semaphore()

    def signal(semaphore, member, r):
        pl.semaphore_signal(semaphore, inc=1, device_id=(member, r), device_id_type=MESH)

    def at_sides(below, above):
        pl.when(has_lower)(below)
        pl.when(has_upper)(above)

    def greet_side(r):
        signal(barrier, me, r)
        signal(barrier, other, r)

    at_sides(lambda: greet_side(lower), lambda: greet_side(upper))
    steps_y = [lax.rem(ry + step, tall) for step in (1, tall - 1)]
    next_x = [lax.rem(rx + step, wide) * deep + rz for step in (1, wide - 1)]
    for y in steps_y:
        for c in range(CORES):
            signal(barrier, y * CORES + c, region)
    for r in next_x:
        signal(barrier, me, r)
    signal(barrier, other, region)

    load_lat = load(latent_in, lat, 0)
    load_wk = load_columns(wk_in, wk, 1)
    load_wv = load_columns(wv_in, wv, 3)

    def remote(src, dst, send_sem, recv_sem, member, r):
        return pltpu.make_async_remote_copy(
            src_ref=src, dst_ref=dst, send_sem=send_sem, recv_sem=recv_sem,
            device_id=(member, r), device_id_type=MESH,
        )

    def send(*what):
        copy = remote(*what)
        copy.start()
        return copy

    def drain(bytes_of, semaphore):
        pltpu.make_async_copy(bytes_of, bytes_of, semaphore).wait()

    def swap(low_src, low_dst, up_src, up_dst, sems, k=0):
        down = remote(low_src, low_dst, sems[0].at[k], sems[1].at[k], me, lower)
        up = remote(up_src, up_dst, sems[0].at[k + 1], sems[1].at[k + 1], me, upper)
        at_sides(down.start, up.start)

        def below():
            down.wait_send()
            up.wait_recv()

        def above():
            up.wait_send()
            down.wait_recv()

        def finish():
            at_sides(below, above)

        return finish

    load_lat.wait()
    for g in range(groups):
        cols = pl.ds(g * GROUP, GROUP)
        for i, (loads, w) in enumerate(((load_wk, wk), (load_wv, wv))):
            if g % 2 == 0:
                loads[g // 2].wait()
            if g == groups - 2 and i == 0:
                load_feats = load(feats_in, feats, 5)
                load_wq = load_columns(wq_in, wq, 6)
                load_edges = load(edges_in, edges, 8)
                load_wo = load(wo_in, wo, 9)
                load_target = load(target_in, target, 10)
            kv[i, :, cols] = jnp.dot(lat[...], w[:, cols], preferred_element_type=F32)
    for side, row in enumerate((0, own_nodes - HALO)):
        rim_out[side] = jnp.concatenate(
            [kv[0, pl.ds(row, HALO), :], kv[1, pl.ds(row, HALO), :]], axis=0
        ).astype(BF16)
    @pl.when(jnp.logical_not(has_lower))
    def _():
        rim_in[0] = jnp.zeros(rim_in.shape[1:], BF16)
        halo[0] = jnp.zeros(halo.shape[1:], F32)

    @pl.when(jnp.logical_not(has_upper))
    def _():
        rim_in[1] = jnp.zeros(rim_in.shape[1:], BF16)
        halo[1] = jnp.zeros(halo.shape[1:], F32)

    sides = has_lower.astype(jnp.int32) + has_upper.astype(jnp.int32)
    pl.semaphore_wait(barrier, 2 * CORES + 2 + 1 + CORES * sides)
    rims = swap(rim_out.at[0], rim_in.at[1], rim_out.at[1], rim_in.at[0], (rim_send, rim_recv))

    for y in steps_y:
        signal(hello_one, y * CORES + rc, region)
    for r in next_x:
        signal(hello_one, me, r)

    load_feats.wait()
    for g in range(groups):
        cols = pl.ds(g * GROUP, GROUP)
        if g % 2 == 0:
            load_wq[g // 2].wait()
        query[:, cols] = jnp.dot(
            feats[...], wq[:, cols], preferred_element_type=F32
        ).astype(BF16)

    load_edges.wait()
    links = edges[...] - region * own_nodes
    links = jnp.where(links < 0, links + window, links)
    node = lax.broadcasted_iota(jnp.int32, (window, points), 0)
    node = jnp.where(node < own_nodes, node, jnp.where(node < own_nodes + HALO, node + HALO, node - HALO))
    count = jnp.zeros((window, points), F32)
    for e in range(edges_in.shape[0]):
        count = count + jnp.where(node == links[e : e + 1, :], 1.0, 0.0)
    linked = count > 0.0

    def head_of(rows):
        return lax.broadcasted_iota(jnp.int32, (rows, GROUP), 1) // head_size

    def spread(x, h):
        return jnp.where(head_of(x.shape[0]) == h, x, 0.0).astype(BF16)

    def gather(x):
        own, rim = x[:own_nodes], x[heads * own_nodes : heads * own_nodes + 2 * HALO]
        for h in range(1, heads):
            at = heads * own_nodes + h * 2 * HALO
            own = jnp.where(head_of(own_nodes) == h, x[h * own_nodes : (h + 1) * own_nodes], own)
            rim = jnp.where(head_of(2 * HALO) == h, x[at : at + 2 * HALO], rim)
        return jnp.concatenate([own, rim], axis=0)

    def fold(op, reduce, own, rim):
        pieces = [x[i : i + 8] for x in (own, rim) for i in range(0, x.shape[0], 8)]
        while len(pieces) > 1:
            pieces = [op(*pair) for pair in zip(pieces[::2], pieces[1::2])] + pieces[len(pieces) // 2 * 2 :]
        return reduce(pieces[0], axis=0, keepdims=True)

    stacked = heads * own_nodes
    for g in range(groups):
        cols = pl.ds(g * GROUP, GROUP)
        kb = jnp.concatenate([spread(kv[0, :, cols], h) for h in range(heads)], axis=0)
        vb = jnp.concatenate([spread(kv[1, :, cols], h) for h in range(heads)], axis=0)
        vbd[g, pl.ds(0, stacked), :] = vb
        vt[g, :, pl.ds(0, stacked)] = vb.T
        own = lax.dot_general(kb, query[:, cols], NT, preferred_element_type=F32)
        for h in range(heads):
            rows = slice(h * own_nodes, (h + 1) * own_nodes)
            scores[g, rows, :] = jnp.where(linked[:own_nodes], own[rows], -jnp.inf)

    load_target.wait()
    load_wo.wait()
    tpad[...] = jnp.zeros_like(tpad)
    tpad[pl.ds(0, variables), :] = target[...]
    wof[...] = jnp.zeros_like(wof)
    wof[pl.ds(0, variables), :] = wo[...].astype(F32)
    won[...] = wof[...].T.astype(BF16)
    pred[...] = jnp.zeros_like(pred)

    rims()
    def along(semaphore, z):
        for c in range(CORES):
            signal(semaphore, ry * CORES + c, rx * deep + z)

    pl.when(rz >= 2)(lambda: along(hello_two, rz - 2))
    pl.when(rz < deep - 2)(lambda: along(hello_two, rz + 2))
    rim_scores = []
    for g in range(groups):
        cols = pl.ds(g * GROUP, GROUP)
        both = [
            jnp.concatenate(
                [rim_in[side, :, cols].astype(F32)[i * HALO : (i + 1) * HALO] for side in range(2)], axis=0
            )
            for i in range(2)
        ]
        kb = jnp.concatenate([spread(both[0], h) for h in range(heads)], axis=0)
        vb = jnp.concatenate([spread(both[1], h) for h in range(heads)], axis=0)
        rim_scores.append(lax.dot_general(kb, query[:, cols], NT, preferred_element_type=F32))
        vbd[g, pl.ds(stacked, heads * 2 * HALO), :] = vb
        vt[g, :, pl.ds(stacked, heads * 2 * HALO)] = vb.T
    scale = head_size ** (-0.5)

    def attend(g):
        parts, rim_parts = [], []
        for h in range(heads):
            rows = pl.ds(h * own_nodes, own_nodes)
            s = scores[g, rows, :]
            r = jnp.where(linked[own_nodes:], rim_scores[g][h * 2 * HALO : (h + 1) * 2 * HALO], -jnp.inf)
            top = fold(jnp.maximum, jnp.max, s, r)
            e = count[:own_nodes] * jnp.exp2((s - top) * (scale * LOG2E))
            f = count[own_nodes:] * jnp.exp2((r - top) * (scale * LOG2E))
            inv = 1.0 / fold(jnp.add, jnp.sum, e, f)
            e, f = e * inv, f * inv
            attn[g, rows, :] = e
            attn[g, pl.ds(stacked + h * 2 * HALO, 2 * HALO), :] = f
            parts.append(e.astype(BF16))
            rim_parts.append(f.astype(BF16))
        a16 = jnp.concatenate(parts + rim_parts, axis=0)
        attn16[g] = a16
        return a16

    total = jnp.zeros((variables, points), F32)
    weights, contexts = {}, {}
    for step in range(groups + 2):
        if step < groups:
            weights[step] = attend(step)
        if 0 <= step - 1 < groups:
            contexts[step - 1] = jnp.dot(vt[step - 1], weights[step - 1], preferred_element_type=F32).astype(BF16)
        if 0 <= step - 2:
            g = step - 2
            total = total + jnp.dot(wo[:, pl.ds(g * GROUP, GROUP)], contexts[g], preferred_element_type=F32)
    pred[pl.ds(0, variables), :] = total

    pl.semaphore_wait(hello_one, 4)
    for k in order:
        send(pred.at[pl.ds(pl.multiple_of(peers[k] * ROWS, ROWS), ROWS)], got.at[k],
             go_send, go_recv, peers[k], region)
    first = pl.multiple_of(me * ROWS, ROWS)
    got[0] = pred[pl.ds(first, ROWS), :]
    drain(got.at[pl.ds(1, members - 1)], go_send)
    drain(got.at[pl.ds(1, members - 1)], go_recv)
    pl.semaphore_wait(hello_two, CORES * ((rz >= 2).astype(jnp.int32) + (rz < deep - 2).astype(jnp.int32)))
    along(hello_four, lax.rem(rz + 4, deep))

    coeff = 1.0 - (1.0 - ALPHA) / members
    pair = coeff / (members * (members - 1))
    loss_part = jnp.zeros((8, 128), F32)
    for top in range(0, ROWS, 8):
        row = lax.broadcasted_iota(jnp.int32, (8, 128), 0) + first + top
        valid = row < variables
        block_loss = jnp.zeros((8, 128), F32)
        for left in range(0, points, 128):
            at = (pl.ds(top, 8), pl.ds(left, 128))
            goal = tpad[pl.ds(first + top, 8), pl.ds(left, 128)]
            ps = [got[(k,) + at] for k in range(members)]
            slopes = [None] * members
            near = jnp.zeros((8, 128), F32)
            apart = jnp.full((8, 128), 0.5 * members * math.sqrt(DELTA_SQ), F32)
            grads = []
            for i in range(members):
                d = ps[i] - goal
                sq = d * d + DELTA_SQ
                inv = lax.rsqrt(sq)
                near = near + sq * inv
                grads.append(d * inv)
            for i in range(members):
                for j in range(i + 1, members):
                    d = ps[i] - ps[j]
                    sq = d * d + DELTA_SQ
                    inv = lax.rsqrt(sq)
                    apart = apart + sq * inv
                    d = d * inv
                    slopes[i] = d if slopes[i] is None else slopes[i] + d
                    slopes[j] = -d if slopes[j] is None else slopes[j] - d
            block_loss = block_loss + (near * (1.0 / members) - apart * pair)
            for i in range(members):
                back_out[(i,) + at] = (grads[i] * (1.0 / members) - slopes[i] * pair).astype(BF16)
        loss_part = loss_part + jnp.where(valid, block_loss, 0.0)

    loss_part = jnp.sum(loss_part, axis=0, keepdims=True)
    mine[0] = loss_part
    slot = rx * tall + ry
    plane_loss[slot] = loss_part
    for _, m, r in plane:
        send(mine.at[0], plane_loss.at[slot], pl_send, pl_recv, m, r)
    for k in order:
        owner = lax.rem(me + members - k, members)
        send(back_out.at[k], back.at[pl.ds(first, ROWS)], ret_send, ret_recv, owner, region)
    back[pl.ds(first, ROWS), :] = back_out[0]

    drain(plane_loss.at[pl.ds(1, len(plane))], pl_send)
    drain(plane_loss.at[pl.ds(1, len(plane))], pl_recv)
    pl.semaphore_wait(hello_four, CORES)
    loss_part = plane_loss[0]
    for k in range(1, wide * tall):
        loss_part = loss_part + plane_loss[k]
    loss_part = jnp.broadcast_to(jnp.sum(loss_part, axis=1, keepdims=True) * (1.0 / npts), loss_part.shape)
    mine[1] = loss_part
    slot = rz * CORES + rc
    deep_loss[slot] = loss_part
    for _, m, r in line:
        send(mine.at[1], deep_loss.at[slot], dl_send, dl_recv, m, r)

    drain(back_out.at[pl.ds(1, members - 1)], ret_send)
    drain(back_out.at[pl.ds(1, members - 1)], ret_recv)
    gcs, gas, gk, gv = [], [], [], []
    for g in range(groups):
        gc = jnp.dot(won[pl.ds(g * GROUP, GROUP), :], back[...], preferred_element_type=F32).astype(BF16)
        gcs.append(gc)
    for g in range(groups):
        gas.append(jnp.dot(vbd[g], gcs[g], preferred_element_type=F32))
    for g in range(groups):
        gv.append(gather(lax.dot_general(attn16[g], gcs[g], NT, preferred_element_type=F32)).astype(BF16))
    for g in range(groups):
        cols = pl.ds(g * GROUP, GROUP)
        ga = gas[g]
        parts, rim_parts = [], []
        for h in range(heads):
            at = stacked + h * 2 * HALO
            a, f = attn[g, pl.ds(h * own_nodes, own_nodes), :], attn[g, pl.ds(at, 2 * HALO), :]
            t, u = a * ga[h * own_nodes : (h + 1) * own_nodes], f * ga[at : at + 2 * HALO]
            mean = fold(jnp.add, jnp.sum, t, u)
            parts.append(t - a * mean)
            rim_parts.append(u - f * mean)
        gs = jnp.concatenate(parts + rim_parts, axis=0).astype(BF16)
        gk.append((gather(jnp.dot(gs, query[:, cols], preferred_element_type=F32)) * scale).astype(BF16))
    gk = jnp.concatenate(gk, axis=1)
    gv = jnp.concatenate(gv, axis=1)

    for c in range(width // GROUP):
        cols = pl.ds(c * GROUP, GROUP)
        out = lax.dot_general(gk, wk[cols, :], NT, preferred_element_type=F32)
        out = out + lax.dot_general(gv, wv[cols, :], NT, preferred_element_type=F32)
        gl[:, cols] = out[own_nodes:]
        grad_out[:, cols] = out[:own_nodes]
    rims = swap(
        gl.at[pl.ds(0, HALO)], halo.at[1], gl.at[pl.ds(HALO, HALO)], halo.at[0], (halo_send, halo_recv)
    )
    rims()
    grad_out[pl.ds(0, HALO), :] += halo[0]
    grad_out[pl.ds(own_nodes - HALO, HALO), :] += halo[1]

    drain(deep_loss.at[pl.ds(1, len(line))], dl_send)
    drain(deep_loss.at[pl.ds(1, len(line))], dl_recv)
    loss_part = deep_loss[0]
    for k in range(1, deep * CORES):
        loss_part = loss_part + deep_loss[k]
    loss_out[...] = jnp.broadcast_to(loss_part, loss_out.shape)


def finish(grad, loss, grad_out, loss_out, one, sem):
    copies = [pltpu.make_async_copy(grad, grad_out, sem.at[0]), pltpu.make_async_copy(one, loss_out, sem.at[1])]
    copies[0].start()
    one[...] = loss[pl.ds(0, 1), pl.ds(0, 1)]
    copies[1].start()
    for copy in copies:
        copy.wait()


def local(members, regions, mesh_latent, grid_feat, edges, target, w_query, w_key, w_value, w_out):
    latent = mesh_latent[0]
    feats = grid_feat[0]
    own_nodes, width = latent.shape
    points, links = edges.shape
    variables = target.shape[1]
    window = own_nodes + 2 * HALO
    deep = math.gcd(regions, 8) if regions > 8 else 2
    wide, tall = regions // deep, members // CORES
    groups = width // GROUP
    stack = window * GROUP // (width // HEADS)
    padded = members * ROWS
    dma = pltpu.SemaphoreType.DMA
    any_space = pl.BlockSpec(memory_space=pltpu.HBM)
    vmem = pl.BlockSpec(memory_space=pltpu.VMEM)
    grad, loss = pl.pallas_call(
        functools.partial(kernel, members, regions, deep, points * regions * variables),
        out_shape=(
            jax.ShapeDtypeStruct((own_nodes, width), F32),
            jax.ShapeDtypeStruct((8, 128), F32),
        ),
        in_specs=[any_space] * 8,
        out_specs=(vmem, vmem),
        scratch_shapes=[
            pltpu.VMEM((own_nodes, width), BF16),
            pltpu.VMEM((points, width), BF16),
            pltpu.VMEM((links, points), jnp.int32),
            pltpu.VMEM((variables, points), F32),
            pltpu.VMEM((width, width), BF16),
            pltpu.VMEM((width, width), BF16),
            pltpu.VMEM((width, width), BF16),
            pltpu.VMEM((variables, width), BF16),
            pltpu.VMEM((2, own_nodes, width), F32),
            pltpu.VMEM((2, 2 * HALO, width), BF16),
            pltpu.VMEM((2, 2 * HALO, width), BF16),
            pltpu.VMEM((padded, points), F32),
            pltpu.VMEM((padded, width), F32),
            pltpu.VMEM((width, padded), BF16),
            pltpu.VMEM((points, width), BF16),
            pltpu.VMEM((groups, stack, points), F32),
            pltpu.VMEM((groups, GROUP, stack), BF16),
            pltpu.VMEM((groups, stack, GROUP), BF16),
            pltpu.VMEM((groups, stack, points), F32),
            pltpu.VMEM((groups, stack, points), BF16),
            pltpu.VMEM((padded, points), F32),
            pltpu.VMEM((members, ROWS, points), F32),
            pltpu.VMEM((members, ROWS, points), BF16),
            pltpu.VMEM((padded, points), BF16),
            pltpu.VMEM((2 * HALO, width), F32),
            pltpu.VMEM((2, HALO, width), F32),
            pltpu.VMEM((wide * tall, 1, 128), F32),
            pltpu.VMEM((deep * CORES, 1, 128), F32),
            pltpu.VMEM((2, 1, 128), F32),
            pltpu.SemaphoreType.REGULAR,
            pltpu.SemaphoreType.REGULAR,
            pltpu.SemaphoreType.REGULAR,
            dma((11,)),
            dma((2,)), dma((2,)),
            dma, dma,
            dma, dma,
            dma((2,)), dma((2,)),
            dma, dma,
            dma, dma,
        ],
        compiler_params=pltpu.CompilerParams(
            collective_id=0, has_side_effects=True, vmem_limit_bytes=24 * 1024 * 1024
        ),
    )(*[pltpu.with_memory_space_constraint(x, pltpu.HBM) for x in (latent, feats, edges.T, target.T, w_query, w_key, w_value, w_out.T)])
    grad, loss = pl.pallas_call(
        finish,
        out_shape=(
            jax.ShapeDtypeStruct((own_nodes, width), F32),
            jax.ShapeDtypeStruct((1, 1), F32),
        ),
        in_specs=[vmem, vmem],
        out_specs=(pl.BlockSpec(memory_space=pltpu.HBM), pl.BlockSpec(memory_space=pltpu.HBM)),
        scratch_shapes=[pltpu.VMEM((1, 1), F32), dma((2,))],
        compiler_params=pltpu.CompilerParams(vmem_limit_bytes=4 * 1024 * 1024),
    )(grad, loss)
    return grad[None], loss[0, 0]


def solution(mesh):
    in_specs = (
        P("ens", "grid", None),
        P("ens", "grid", None),
        P("grid", None),
        P("grid", None),
        P(),
        P(),
        P(),
        P(),
    )
    out_specs = (P("ens", "grid", None), P())
    return jax.shard_map(
        functools.partial(local, mesh.shape["ens"], mesh.shape["grid"]),
        mesh=mesh, in_specs=in_specs, out_specs=out_specs, check_vma=False,
    )
```

```python
import functools
import math

import jax
import jax.numpy as jnp
from jax import lax
from jax.experimental import pallas as pl
from jax.experimental.pallas import tpu as pltpu
from jax.sharding import PartitionSpec as P

HEADS = 16
HALO = 8
DELTA_SQ = 0.01
ALPHA = 0.95
LOG2E = math.log2(math.e)

MESH = pl.DeviceIdType.MESH
F32 = jnp.float32
BF16 = jnp.bfloat16

CORES = 2
ROWS = 16
GROUP = 256
NT = (((1,), (1,)), ((), ()))
TN = (((0,), (0,)), ((), ()))


def kernel(
    members, regions, deep, npts,
    latent_in, feats_in, edges_in, target_in, wq_in, wk_in, wv_in, wo_in,
    grad_out, loss_out,
    lat, feats, edges, target, wq, wk, wv, wo,
    kv, rim_out, rim_in, tpad, wof, won, query, scores, tops, sums, vt, vbd, attn, attn16, pred, got, back_out, back,
    gl, halo, plane_loss, deep_loss, mine,
    hello_one, hello_two, hello_four, load_sem, rim_send, rim_recv, go_send, go_recv, ret_send, ret_recv,
    halo_send, halo_recv, pl_send, pl_recv, dl_send, dl_recv,
):
    me = lax.axis_index("ens")
    region = lax.axis_index("grid")
    wide, tall = regions // deep, members // CORES
    rx, rz = region // deep, lax.rem(region, deep)
    ry, rc = me // CORES, lax.rem(me, CORES)
    own_nodes, width = latent_in.shape
    points = feats_in.shape[0]
    variables = wo_in.shape[0]
    window = own_nodes + 2 * HALO
    head_size = width // HEADS
    heads = GROUP // head_size
    groups = width // GROUP
    lower = lax.rem(region + regions - 1, regions)
    upper = lax.rem(region + 1, regions)
    peers = [lax.rem(me + k, members) for k in range(members)]
    order = sorted(range(1, members), key=lambda k: -min(k // CORES, tall - k // CORES))
    plane, line = [], []
    def far(i, inner, outer):
        return -min(i // inner, outer - i // inner) - (min(i % inner, inner - i % inner) if inner > CORES else 0)

    for i in sorted(range(1, wide * tall), key=lambda i: far(i, tall, wide)):
        x, y = lax.rem(rx + i // tall, wide), lax.rem(ry + i % tall, tall)
        plane.append((i // tall, y * CORES + rc, x * deep + rz))
    for i in sorted(range(1, deep * CORES), key=lambda i: far(i, CORES, deep)):
        z, c = lax.rem(rz + i // CORES, deep), lax.rem(rc + i % CORES, CORES)
        line.append((i // CORES, ry * CORES + c, rx * deep + z))

    def load(src, dst, k):
        copy = pltpu.make_async_copy(src, dst, load_sem.at[k])
        copy.start()
        return copy

    def load_columns(src, dst, k):
        half = width // 2
        return [
            load(src.at[:, pl.ds(i * half, half)], dst.at[:, pl.ds(i * half, half)], k + i) for i in range(2)
        ]

    has_lower, has_upper = region > 0, region < regions - 1
    other = ry * CORES + lax.rem(rc + 1, CORES)
    barrier = pltpu.get_barrier_semaphore()

    def signal(semaphore, member, r):
        pl.semaphore_signal(semaphore, inc=1, device_id=(member, r), device_id_type=MESH)

    def at_sides(below, above):
        pl.when(has_lower)(below)
        pl.when(has_upper)(above)

    def greet_side(r):
        signal(barrier, me, r)
        signal(barrier, other, r)

    at_sides(lambda: greet_side(lower), lambda: greet_side(upper))
    steps_y = [lax.rem(ry + step, tall) for step in (1, tall - 1)]
    next_x = [lax.rem(rx + step, wide) * deep + rz for step in (1, wide - 1)]
    for y in steps_y:
        for c in range(CORES):
            signal(barrier, y * CORES + c, region)
    for r in next_x:
        signal(barrier, me, r)
    signal(barrier, other, region)

    load_lat = load(latent_in, lat, 0)
    load_wk = load_columns(wk_in, wk, 1)
    load_wv = load_columns(wv_in, wv, 3)

    def remote(src, dst, send_sem, recv_sem, member, r):
        return pltpu.make_async_remote_copy(
            src_ref=src, dst_ref=dst, send_sem=send_sem, recv_sem=recv_sem,
            device_id=(member, r), device_id_type=MESH,
        )

    def send(*what):
        copy = remote(*what)
        copy.start()
        return copy

    def drain(bytes_of, semaphore):
        pltpu.make_async_copy(bytes_of, bytes_of, semaphore).wait()

    def swap(low_src, low_dst, up_src, up_dst, sems, k=0):
        down = remote(low_src, low_dst, sems[0].at[k], sems[1].at[k], me, lower)
        up = remote(up_src, up_dst, sems[0].at[k + 1], sems[1].at[k + 1], me, upper)
        at_sides(down.start, up.start)

        def below():
            down.wait_send()
            up.wait_recv()

        def above():
            up.wait_send()
            down.wait_recv()

        def finish():
            at_sides(below, above)

        return finish

    load_lat.wait()
    for g in range(groups):
        cols = pl.ds(g * GROUP, GROUP)
        for i, (loads, w) in enumerate(((load_wk, wk), (load_wv, wv))):
            if g % 2 == 0:
                loads[g // 2].wait()
            if g == groups - 2 and i == 0:
                load_feats = load(feats_in, feats, 5)
                load_wq = load_columns(wq_in, wq, 6)
                load_edges = load(edges_in, edges, 8)
                load_wo = load(wo_in, wo, 9)
                load_target = load(target_in, target, 10)
            kv[i, :, cols] = jnp.dot(lat[...], w[:, cols], preferred_element_type=F32)
    for side, row in enumerate((0, own_nodes - HALO)):
        rim_out[side] = jnp.concatenate(
            [kv[0, pl.ds(row, HALO), :], kv[1, pl.ds(row, HALO), :]], axis=0
        ).astype(BF16)
    @pl.when(jnp.logical_not(has_lower))
    def _():
        rim_in[0] = jnp.zeros(rim_in.shape[1:], BF16)
        halo[0] = jnp.zeros(halo.shape[1:], F32)

    @pl.when(jnp.logical_not(has_upper))
    def _():
        rim_in[1] = jnp.zeros(rim_in.shape[1:], BF16)
        halo[1] = jnp.zeros(halo.shape[1:], F32)

    sides = has_lower.astype(jnp.int32) + has_upper.astype(jnp.int32)
    pl.semaphore_wait(barrier, 2 * CORES + 2 + 1 + CORES * sides)
    rims = swap(rim_out.at[0], rim_in.at[1], rim_out.at[1], rim_in.at[0], (rim_send, rim_recv))

    for y in steps_y:
        signal(hello_one, y * CORES + rc, region)
    for r in next_x:
        signal(hello_one, me, r)

    load_feats.wait()
    for g in range(groups):
        cols = pl.ds(g * GROUP, GROUP)
        if g % 2 == 0:
            load_wq[g // 2].wait()
        query[:, cols] = jnp.dot(
            feats[...], wq[:, cols], preferred_element_type=F32
        ).astype(BF16)

    load_edges.wait()
    links = edges[...] - region * own_nodes
    links = jnp.where(links < 0, links + window, links)
    node = lax.broadcasted_iota(jnp.int32, (window, points), 0)
    node = jnp.where(node < own_nodes, node, jnp.where(node < own_nodes + HALO, node + HALO, node - HALO))
    count = jnp.zeros((window, points), F32)
    for e in range(edges_in.shape[0]):
        count = count + jnp.where(node == links[e : e + 1, :], 1.0, 0.0)
    linked = count > 0.0

    def head_of(rows):
        return lax.broadcasted_iota(jnp.int32, (rows, GROUP), 1) // head_size

    def spread(x, h):
        return jnp.where(head_of(x.shape[0]) == h, x, 0.0).astype(BF16)

    def gather(x):
        own, rim = x[:own_nodes], x[heads * own_nodes : heads * own_nodes + 2 * HALO]
        for h in range(1, heads):
            at = heads * own_nodes + h * 2 * HALO
            own = jnp.where(head_of(own_nodes) == h, x[h * own_nodes : (h + 1) * own_nodes], own)
            rim = jnp.where(head_of(2 * HALO) == h, x[at : at + 2 * HALO], rim)
        return jnp.concatenate([own, rim], axis=0)

    def fold(op, reduce, *arrays):
        pieces = [x[i : i + 8] for x in arrays for i in range(0, x.shape[0], 8)]
        while len(pieces) > 1:
            pieces = [op(*pair) for pair in zip(pieces[::2], pieces[1::2])] + pieces[len(pieces) // 2 * 2 :]
        return reduce(pieces[0], axis=0, keepdims=True)

    scale = head_size ** (-0.5)
    stacked = heads * own_nodes
    for g in range(groups):
        cols = pl.ds(g * GROUP, GROUP)
        kb = jnp.concatenate([spread(kv[0, :, cols], h) for h in range(heads)], axis=0)
        vb = jnp.concatenate([spread(kv[1, :, cols], h) for h in range(heads)], axis=0)
        vbd[g, pl.ds(0, stacked), :] = vb
        vt[g, :, pl.ds(0, stacked)] = vb.T
        own = lax.dot_general(kb, query[:, cols], NT, preferred_element_type=F32)
        for h in range(heads):
            rows = slice(h * own_nodes, (h + 1) * own_nodes)
            s = jnp.where(linked[:own_nodes], own[rows], -jnp.inf)
            top = jnp.maximum(fold(jnp.maximum, jnp.max, s), -1e30)
            e = count[:own_nodes] * jnp.exp2((s - top) * (scale * LOG2E))
            scores[g, rows, :] = e
            tops[g * heads + h] = top
            sums[g * heads + h] = fold(jnp.add, jnp.sum, e)

    load_target.wait()
    load_wo.wait()
    tpad[...] = jnp.zeros_like(tpad)
    tpad[pl.ds(0, variables), :] = target[...]
    wof[...] = jnp.zeros_like(wof)
    wof[pl.ds(0, variables), :] = wo[...].astype(F32)
    won[...] = wof[...].T.astype(BF16)
    pred[...] = jnp.zeros_like(pred)

    rims()
    def along(semaphore, z):
        for c in range(CORES):
            signal(semaphore, ry * CORES + c, rx * deep + z)

    pl.when(rz >= 2)(lambda: along(hello_two, rz - 2))
    pl.when(rz < deep - 2)(lambda: along(hello_two, rz + 2))
    rim_scores = []
    for g in range(groups):
        cols = pl.ds(g * GROUP, GROUP)
        both = [
            jnp.concatenate(
                [rim_in[side, :, cols].astype(F32)[i * HALO : (i + 1) * HALO] for side in range(2)], axis=0
            )
            for i in range(2)
        ]
        kb = jnp.concatenate([spread(both[0], h) for h in range(heads)], axis=0)
        vb = jnp.concatenate([spread(both[1], h) for h in range(heads)], axis=0)
        rim_scores.append(lax.dot_general(kb, query[:, cols], NT, preferred_element_type=F32))
        vbd[g, pl.ds(stacked, heads * 2 * HALO), :] = vb
        vt[g, :, pl.ds(stacked, heads * 2 * HALO)] = vb.T
    def attend(g):
        parts, rim_parts = [], []
        for h in range(heads):
            rows = pl.ds(h * own_nodes, own_nodes)
            own_top = tops[g * heads + h]
            r = jnp.where(linked[own_nodes:], rim_scores[g][h * 2 * HALO : (h + 1) * 2 * HALO], -jnp.inf)
            top = jnp.maximum(own_top, fold(jnp.maximum, jnp.max, r))
            weight = jnp.exp2((own_top - top) * (scale * LOG2E))
            f = count[own_nodes:] * jnp.exp2((r - top) * (scale * LOG2E))
            inv = 1.0 / (sums[g * heads + h] * weight + fold(jnp.add, jnp.sum, f))
            e, f = scores[g, rows, :] * (weight * inv), f * inv
            attn[g, rows, :] = e
            attn[g, pl.ds(stacked + h * 2 * HALO, 2 * HALO), :] = f
            parts.append(e.astype(BF16))
            rim_parts.append(f.astype(BF16))
        a16 = jnp.concatenate(parts + rim_parts, axis=0)
        attn16[g] = a16
        return a16

    total = jnp.zeros((variables, points), F32)
    weights, contexts = {}, {}
    for step in range(groups + 2):
        if step < groups:
            weights[step] = attend(step)
        if 0 <= step - 1 < groups:
            contexts[step - 1] = jnp.dot(vt[step - 1], weights[step - 1], preferred_element_type=F32).astype(BF16)
        if 0 <= step - 2:
            g = step - 2
            total = total + jnp.dot(wo[:, pl.ds(g * GROUP, GROUP)], contexts[g], preferred_element_type=F32)
    pred[pl.ds(0, variables), :] = total

    pl.semaphore_wait(hello_one, 4)
    for k in order:
        send(pred.at[pl.ds(pl.multiple_of(peers[k] * ROWS, ROWS), ROWS)], got.at[k],
             go_send, go_recv, peers[k], region)
    first = pl.multiple_of(me * ROWS, ROWS)
    got[0] = pred[pl.ds(first, ROWS), :]
    drain(got.at[pl.ds(1, members - 1)], go_send)
    drain(got.at[pl.ds(1, members - 1)], go_recv)
    pl.semaphore_wait(hello_two, CORES * ((rz >= 2).astype(jnp.int32) + (rz < deep - 2).astype(jnp.int32)))
    along(hello_four, lax.rem(rz + 4, deep))

    coeff = 1.0 - (1.0 - ALPHA) / members
    pair = coeff / (members * (members - 1))
    loss_part = jnp.zeros((8, 128), F32)
    for top in range(0, ROWS, 8):
        row = lax.broadcasted_iota(jnp.int32, (8, 128), 0) + first + top
        valid = row < variables
        block_loss = jnp.zeros((8, 128), F32)
        for left in range(0, points, 128):
            at = (pl.ds(top, 8), pl.ds(left, 128))
            goal = tpad[pl.ds(first + top, 8), pl.ds(left, 128)]
            ps = [got[(k,) + at] for k in range(members)]
            slopes = [None] * members
            near = jnp.zeros((8, 128), F32)
            apart = jnp.full((8, 128), 0.5 * members * math.sqrt(DELTA_SQ), F32)
            grads = []
            for i in range(members):
                d = ps[i] - goal
                sq = d * d + DELTA_SQ
                inv = lax.rsqrt(sq)
                near = near + sq * inv
                grads.append(d * inv)
            for i in range(members):
                for j in range(i + 1, members):
                    d = ps[i] - ps[j]
                    sq = d * d + DELTA_SQ
                    inv = lax.rsqrt(sq)
                    apart = apart + sq * inv
                    d = d * inv
                    slopes[i] = d if slopes[i] is None else slopes[i] + d
                    slopes[j] = -d if slopes[j] is None else slopes[j] - d
            block_loss = block_loss + (near * (1.0 / members) - apart * pair)
            for i in range(members):
                back_out[(i,) + at] = (grads[i] * (1.0 / members) - slopes[i] * pair).astype(BF16)
        loss_part = loss_part + jnp.where(valid, block_loss, 0.0)

    loss_part = jnp.sum(loss_part, axis=0, keepdims=True)
    mine[0] = loss_part
    slot = rx * tall + ry
    plane_loss[slot] = loss_part
    for _, m, r in plane:
        send(mine.at[0], plane_loss.at[slot], pl_send, pl_recv, m, r)
    for k in order:
        owner = lax.rem(me + members - k, members)
        send(back_out.at[k], back.at[pl.ds(first, ROWS)], ret_send, ret_recv, owner, region)
    back[pl.ds(first, ROWS), :] = back_out[0]

    drain(plane_loss.at[pl.ds(1, len(plane))], pl_send)
    drain(plane_loss.at[pl.ds(1, len(plane))], pl_recv)
    pl.semaphore_wait(hello_four, CORES)
    loss_part = plane_loss[0]
    for k in range(1, wide * tall):
        loss_part = loss_part + plane_loss[k]
    loss_part = jnp.broadcast_to(jnp.sum(loss_part, axis=1, keepdims=True) * (1.0 / npts), loss_part.shape)
    mine[1] = loss_part
    slot = rz * CORES + rc
    deep_loss[slot] = loss_part
    for _, m, r in line:
        send(mine.at[1], deep_loss.at[slot], dl_send, dl_recv, m, r)

    drain(back_out.at[pl.ds(1, members - 1)], ret_send)
    drain(back_out.at[pl.ds(1, members - 1)], ret_recv)
    gcs, gas, gk, gv = [], [], [], []
    for g in range(groups):
        gc = jnp.dot(won[pl.ds(g * GROUP, GROUP), :], back[...], preferred_element_type=F32).astype(BF16)
        gcs.append(gc)
    for g in range(groups):
        gas.append(jnp.dot(vbd[g], gcs[g], preferred_element_type=F32))
    for g in range(groups):
        gv.append(gather(lax.dot_general(attn16[g], gcs[g], NT, preferred_element_type=F32)).astype(BF16))
    for g in range(groups):
        cols = pl.ds(g * GROUP, GROUP)
        ga = gas[g]
        parts, rim_parts = [], []
        for h in range(heads):
            at = stacked + h * 2 * HALO
            a, f = attn[g, pl.ds(h * own_nodes, own_nodes), :], attn[g, pl.ds(at, 2 * HALO), :]
            t, u = a * ga[h * own_nodes : (h + 1) * own_nodes], f * ga[at : at + 2 * HALO]
            mean = fold(jnp.add, jnp.sum, t, u)
            parts.append(t - a * mean)
            rim_parts.append(u - f * mean)
        gs = jnp.concatenate(parts + rim_parts, axis=0).astype(BF16)
        gk.append((gather(jnp.dot(gs, query[:, cols], preferred_element_type=F32)) * scale).astype(BF16))
    gk = jnp.concatenate(gk, axis=1)
    gv = jnp.concatenate(gv, axis=1)

    for c in range(width // GROUP):
        cols = pl.ds(c * GROUP, GROUP)
        out = lax.dot_general(gk, wk[cols, :], NT, preferred_element_type=F32)
        out = out + lax.dot_general(gv, wv[cols, :], NT, preferred_element_type=F32)
        gl[:, cols] = out[own_nodes:]
        grad_out[:, cols] = out[:own_nodes]
    rims = swap(
        gl.at[pl.ds(0, HALO)], halo.at[1], gl.at[pl.ds(HALO, HALO)], halo.at[0], (halo_send, halo_recv)
    )
    rims()
    grad_out[pl.ds(0, HALO), :] += halo[0]
    grad_out[pl.ds(own_nodes - HALO, HALO), :] += halo[1]

    drain(deep_loss.at[pl.ds(1, len(line))], dl_send)
    drain(deep_loss.at[pl.ds(1, len(line))], dl_recv)
    loss_part = deep_loss[0]
    for k in range(1, deep * CORES):
        loss_part = loss_part + deep_loss[k]
    loss_out[...] = jnp.broadcast_to(loss_part, loss_out.shape)


def finish(grad, loss, grad_out, loss_out, one, sem):
    copies = [pltpu.make_async_copy(grad, grad_out, sem.at[0]), pltpu.make_async_copy(one, loss_out, sem.at[1])]
    copies[0].start()
    one[...] = loss[pl.ds(0, 1), pl.ds(0, 1)]
    copies[1].start()
    for copy in copies:
        copy.wait()


def local(members, regions, mesh_latent, grid_feat, edges, target, w_query, w_key, w_value, w_out):
    latent = mesh_latent[0]
    feats = grid_feat[0]
    own_nodes, width = latent.shape
    points, links = edges.shape
    variables = target.shape[1]
    window = own_nodes + 2 * HALO
    deep = math.gcd(regions, 8) if regions > 8 else 2
    wide, tall = regions // deep, members // CORES
    groups = width // GROUP
    stack = window * GROUP // (width // HEADS)
    padded = members * ROWS
    dma = pltpu.SemaphoreType.DMA
    any_space = pl.BlockSpec(memory_space=pltpu.HBM)
    vmem = pl.BlockSpec(memory_space=pltpu.VMEM)
    grad, loss = pl.pallas_call(
        functools.partial(kernel, members, regions, deep, points * regions * variables),
        out_shape=(
            jax.ShapeDtypeStruct((own_nodes, width), F32),
            jax.ShapeDtypeStruct((8, 128), F32),
        ),
        in_specs=[any_space] * 8,
        out_specs=(vmem, vmem),
        scratch_shapes=[
            pltpu.VMEM((own_nodes, width), BF16),
            pltpu.VMEM((points, width), BF16),
            pltpu.VMEM((links, points), jnp.int32),
            pltpu.VMEM((variables, points), F32),
            pltpu.VMEM((width, width), BF16),
            pltpu.VMEM((width, width), BF16),
            pltpu.VMEM((width, width), BF16),
            pltpu.VMEM((variables, width), BF16),
            pltpu.VMEM((2, own_nodes, width), F32),
            pltpu.VMEM((2, 2 * HALO, width), BF16),
            pltpu.VMEM((2, 2 * HALO, width), BF16),
            pltpu.VMEM((padded, points), F32),
            pltpu.VMEM((padded, width), F32),
            pltpu.VMEM((width, padded), BF16),
            pltpu.VMEM((points, width), BF16),
            pltpu.VMEM((groups, stack, points), F32),
            pltpu.VMEM((HEADS, 1, points), F32),
            pltpu.VMEM((HEADS, 1, points), F32),
            pltpu.VMEM((groups, GROUP, stack), BF16),
            pltpu.VMEM((groups, stack, GROUP), BF16),
            pltpu.VMEM((groups, stack, points), F32),
            pltpu.VMEM((groups, stack, points), BF16),
            pltpu.VMEM((padded, points), F32),
            pltpu.VMEM((members, ROWS, points), F32),
            pltpu.VMEM((members, ROWS, points), BF16),
            pltpu.VMEM((padded, points), BF16),
            pltpu.VMEM((2 * HALO, width), F32),
            pltpu.VMEM((2, HALO, width), F32),
            pltpu.VMEM((wide * tall, 1, 128), F32),
            pltpu.VMEM((deep * CORES, 1, 128), F32),
            pltpu.VMEM((2, 1, 128), F32),
            pltpu.SemaphoreType.REGULAR,
            pltpu.SemaphoreType.REGULAR,
            pltpu.SemaphoreType.REGULAR,
            dma((11,)),
            dma((2,)), dma((2,)),
            dma, dma,
            dma, dma,
            dma((2,)), dma((2,)),
            dma, dma,
            dma, dma,
        ],
        compiler_params=pltpu.CompilerParams(
            collective_id=0, has_side_effects=True, vmem_limit_bytes=24 * 1024 * 1024
        ),
    )(*[pltpu.with_memory_space_constraint(x, pltpu.HBM) for x in (latent, feats, edges.T, target.T, w_query, w_key, w_value, w_out.T)])
    grad, loss = pl.pallas_call(
        finish,
        out_shape=(
            jax.ShapeDtypeStruct((own_nodes, width), F32),
            jax.ShapeDtypeStruct((1, 1), F32),
        ),
        in_specs=[vmem, vmem],
        out_specs=(pl.BlockSpec(memory_space=pltpu.HBM), pl.BlockSpec(memory_space=pltpu.HBM)),
        scratch_shapes=[pltpu.VMEM((1, 1), F32), dma((2,))],
        compiler_params=pltpu.CompilerParams(vmem_limit_bytes=4 * 1024 * 1024),
    )(grad, loss)
    return grad[None], loss[0, 0]


def solution(mesh):
    in_specs = (
        P("ens", "grid", None),
        P("ens", "grid", None),
        P("grid", None),
        P("grid", None),
        P(),
        P(),
        P(),
        P(),
    )
    out_specs = (P("ens", "grid", None), P())
    return jax.shard_map(
        functools.partial(local, mesh.shape["ens"], mesh.shape["grid"]),
        mesh=mesh, in_specs=in_specs, out_specs=out_specs, check_vma=False,
    )
```

```python
import functools
import math

import jax
import jax.numpy as jnp
from jax import lax
from jax.experimental import pallas as pl
from jax.experimental.pallas import tpu as pltpu
from jax.sharding import PartitionSpec as P

HEADS = 16
HALO = 8
DELTA_SQ = 0.01
ALPHA = 0.95
LOG2E = math.log2(math.e)

MESH = pl.DeviceIdType.MESH
F32 = jnp.float32
BF16 = jnp.bfloat16

CORES = 2
ROWS = 16
GROUP = 256
NT = (((1,), (1,)), ((), ()))
TN = (((0,), (0,)), ((), ()))


def kernel(
    members, regions, deep, npts,
    latent_in, feats_in, edges_in, target_in, wq_in, wk_in, wv_in, wo_in,
    grad_out, loss_out,
    lat, feats, edges, target, wq, wk, wv, wo,
    kv, rim_out, rim_in, tpad, wof, won, query, scores, tops, sums, vt, vbd, attn, attn16, pred, got, back_out, back,
    gl, halo, plane_loss, deep_loss, mine,
    hello_one, hello_two, hello_four, load_sem, rim_send, rim_recv, go_send, go_recv, ret_send, ret_recv,
    halo_send, halo_recv, pl_send, pl_recv, dl_send, dl_recv,
):
    me = lax.axis_index("ens")
    region = lax.axis_index("grid")
    wide, tall = regions // deep, members // CORES
    rx, rz = region // deep, lax.rem(region, deep)
    ry, rc = me // CORES, lax.rem(me, CORES)
    own_nodes, width = latent_in.shape
    points = feats_in.shape[0]
    variables = wo_in.shape[0]
    window = own_nodes + 2 * HALO
    head_size = width // HEADS
    heads = GROUP // head_size
    groups = width // GROUP
    lower = lax.rem(region + regions - 1, regions)
    upper = lax.rem(region + 1, regions)
    peers = [lax.rem(me + k, members) for k in range(members)]
    order = sorted(range(1, members), key=lambda k: -min(k // CORES, tall - k // CORES))
    plane, line = [], []
    def far(i, inner, outer):
        return -min(i // inner, outer - i // inner) - (min(i % inner, inner - i % inner) if inner > CORES else 0)

    for i in sorted(range(1, wide * tall), key=lambda i: far(i, tall, wide)):
        x, y = lax.rem(rx + i // tall, wide), lax.rem(ry + i % tall, tall)
        plane.append((i // tall, y * CORES + rc, x * deep + rz))
    for i in sorted(range(1, deep * CORES), key=lambda i: far(i, CORES, deep)):
        z, c = lax.rem(rz + i // CORES, deep), lax.rem(rc + i % CORES, CORES)
        line.append((i // CORES, ry * CORES + c, rx * deep + z))

    def load(src, dst, k):
        copy = pltpu.make_async_copy(src, dst, load_sem.at[k])
        copy.start()
        return copy

    has_lower, has_upper = region > 0, region < regions - 1
    other = ry * CORES + lax.rem(rc + 1, CORES)
    barrier = pltpu.get_barrier_semaphore()

    def signal(semaphore, member, r):
        pl.semaphore_signal(semaphore, inc=1, device_id=(member, r), device_id_type=MESH)

    def at_sides(below, above):
        pl.when(has_lower)(below)
        pl.when(has_upper)(above)

    def greet_side(r):
        signal(barrier, me, r)
        signal(barrier, other, r)

    at_sides(lambda: greet_side(lower), lambda: greet_side(upper))
    steps_y = [lax.rem(ry + step, tall) for step in (1, tall - 1)]
    next_x = [lax.rem(rx + step, wide) * deep + rz for step in (1, wide - 1)]
    for y in steps_y:
        for c in range(CORES):
            signal(barrier, y * CORES + c, region)
    for r in next_x:
        signal(barrier, me, r)
    signal(barrier, other, region)

    load_lat = load(latent_in, lat, 0)
    load_wk = load(wk_in, wk, 1)
    load_wv = load(wv_in, wv, 2)

    def remote(src, dst, send_sem, recv_sem, member, r):
        return pltpu.make_async_remote_copy(
            src_ref=src, dst_ref=dst, send_sem=send_sem, recv_sem=recv_sem,
            device_id=(member, r), device_id_type=MESH,
        )

    def send(*what):
        copy = remote(*what)
        copy.start()
        return copy

    def drain(bytes_of, semaphore):
        pltpu.make_async_copy(bytes_of, bytes_of, semaphore).wait()

    def swap(low_src, low_dst, up_src, up_dst, sems, k=0):
        down = remote(low_src, low_dst, sems[0].at[k], sems[1].at[k], me, lower)
        up = remote(up_src, up_dst, sems[0].at[k + 1], sems[1].at[k + 1], me, upper)
        at_sides(down.start, up.start)

        def below():
            down.wait_send()
            up.wait_recv()

        def above():
            up.wait_send()
            down.wait_recv()

        def finish():
            at_sides(below, above)

        return finish

    load_lat.wait()
    load_wk.wait()
    load_feats = load(feats_in, feats, 3)
    load_wq = load(wq_in, wq, 4)
    load_edges = load(edges_in, edges, 5)
    load_wo = load(wo_in, wo, 6)
    load_target = load(target_in, target, 7)
    load_wv.wait()
    for g in range(groups):
        cols = pl.ds(g * GROUP, GROUP)
        for i, w in enumerate((wk, wv)):
            kv[i, :, cols] = jnp.dot(lat[...], w[:, cols], preferred_element_type=F32)
    for side, row in enumerate((0, own_nodes - HALO)):
        rim_out[side] = jnp.concatenate(
            [kv[0, pl.ds(row, HALO), :], kv[1, pl.ds(row, HALO), :]], axis=0
        ).astype(BF16)
    @pl.when(jnp.logical_not(has_lower))
    def _():
        rim_in[0] = jnp.zeros(rim_in.shape[1:], BF16)
        halo[0] = jnp.zeros(halo.shape[1:], F32)

    @pl.when(jnp.logical_not(has_upper))
    def _():
        rim_in[1] = jnp.zeros(rim_in.shape[1:], BF16)
        halo[1] = jnp.zeros(halo.shape[1:], F32)

    sides = has_lower.astype(jnp.int32) + has_upper.astype(jnp.int32)
    pl.semaphore_wait(barrier, 2 * CORES + 2 + 1 + CORES * sides)
    rims = swap(rim_out.at[0], rim_in.at[1], rim_out.at[1], rim_in.at[0], (rim_send, rim_recv))

    for y in steps_y:
        signal(hello_one, y * CORES + rc, region)
    for r in next_x:
        signal(hello_one, me, r)

    load_feats.wait()
    load_wq.wait()
    for g in range(groups):
        cols = pl.ds(g * GROUP, GROUP)
        query[:, cols] = jnp.dot(
            feats[...], wq[:, cols], preferred_element_type=F32
        ).astype(BF16)

    load_edges.wait()
    links = edges[...] - region * own_nodes
    links = jnp.where(links < 0, links + window, links)
    node = lax.broadcasted_iota(jnp.int32, (window, points), 0)
    node = jnp.where(node < own_nodes, node, jnp.where(node < own_nodes + HALO, node + HALO, node - HALO))
    count = jnp.zeros((window, points), F32)
    for e in range(edges_in.shape[0]):
        count = count + jnp.where(node == links[e : e + 1, :], 1.0, 0.0)
    linked = count > 0.0

    def head_of(rows):
        return lax.broadcasted_iota(jnp.int32, (rows, GROUP), 1) // head_size

    def spread(x, h):
        return jnp.where(head_of(x.shape[0]) == h, x, 0.0).astype(BF16)

    def gather(x):
        own, rim = x[:own_nodes], x[heads * own_nodes : heads * own_nodes + 2 * HALO]
        for h in range(1, heads):
            at = heads * own_nodes + h * 2 * HALO
            own = jnp.where(head_of(own_nodes) == h, x[h * own_nodes : (h + 1) * own_nodes], own)
            rim = jnp.where(head_of(2 * HALO) == h, x[at : at + 2 * HALO], rim)
        return jnp.concatenate([own, rim], axis=0)

    def fold(op, reduce, *arrays):
        pieces = [x[i : i + 8] for x in arrays for i in range(0, x.shape[0], 8)]
        while len(pieces) > 1:
            pieces = [op(*pair) for pair in zip(pieces[::2], pieces[1::2])] + pieces[len(pieces) // 2 * 2 :]
        return reduce(pieces[0], axis=0, keepdims=True)

    scale = head_size ** (-0.5)
    stacked = heads * own_nodes
    for g in range(groups):
        cols = pl.ds(g * GROUP, GROUP)
        kb = jnp.concatenate([spread(kv[0, :, cols], h) for h in range(heads)], axis=0)
        vb = jnp.concatenate([spread(kv[1, :, cols], h) for h in range(heads)], axis=0)
        vbd[g, pl.ds(0, stacked), :] = vb
        vt[g, :, pl.ds(0, stacked)] = vb.T
        own = lax.dot_general(kb, query[:, cols], NT, preferred_element_type=F32)
        for h in range(heads):
            rows = slice(h * own_nodes, (h + 1) * own_nodes)
            s = jnp.where(linked[:own_nodes], own[rows], -jnp.inf)
            top = jnp.maximum(fold(jnp.maximum, jnp.max, s), -1e30)
            e = count[:own_nodes] * jnp.exp2((s - top) * (scale * LOG2E))
            scores[g, rows, :] = e
            tops[g * heads + h] = top
            sums[g * heads + h] = fold(jnp.add, jnp.sum, e)

    load_target.wait()
    load_wo.wait()
    tpad[...] = jnp.zeros_like(tpad)
    tpad[pl.ds(0, variables), :] = target[...]
    wof[...] = jnp.zeros_like(wof)
    wof[pl.ds(0, variables), :] = wo[...].astype(F32)
    won[...] = wof[...].T.astype(BF16)
    pred[...] = jnp.zeros_like(pred)

    rims()
    def along(semaphore, z):
        for c in range(CORES):
            signal(semaphore, ry * CORES + c, rx * deep + z)

    pl.when(rz >= 2)(lambda: along(hello_two, rz - 2))
    pl.when(rz < deep - 2)(lambda: along(hello_two, rz + 2))
    rim_scores = []
    for g in range(groups):
        cols = pl.ds(g * GROUP, GROUP)
        both = [
            jnp.concatenate(
                [rim_in[side, :, cols].astype(F32)[i * HALO : (i + 1) * HALO] for side in range(2)], axis=0
            )
            for i in range(2)
        ]
        kb = jnp.concatenate([spread(both[0], h) for h in range(heads)], axis=0)
        vb = jnp.concatenate([spread(both[1], h) for h in range(heads)], axis=0)
        rim_scores.append(lax.dot_general(kb, query[:, cols], NT, preferred_element_type=F32))
        vbd[g, pl.ds(stacked, heads * 2 * HALO), :] = vb
        vt[g, :, pl.ds(stacked, heads * 2 * HALO)] = vb.T
    def attend(g):
        parts, rim_parts = [], []
        for h in range(heads):
            rows = pl.ds(h * own_nodes, own_nodes)
            own_top = tops[g * heads + h]
            r = jnp.where(linked[own_nodes:], rim_scores[g][h * 2 * HALO : (h + 1) * 2 * HALO], -jnp.inf)
            top = jnp.maximum(own_top, fold(jnp.maximum, jnp.max, r))
            weight = jnp.exp2((own_top - top) * (scale * LOG2E))
            f = count[own_nodes:] * jnp.exp2((r - top) * (scale * LOG2E))
            inv = 1.0 / (sums[g * heads + h] * weight + fold(jnp.add, jnp.sum, f))
            e, f = scores[g, rows, :] * (weight * inv), f * inv
            attn[g, rows, :] = e
            attn[g, pl.ds(stacked + h * 2 * HALO, 2 * HALO), :] = f
            parts.append(e.astype(BF16))
            rim_parts.append(f.astype(BF16))
        a16 = jnp.concatenate(parts + rim_parts, axis=0)
        attn16[g] = a16
        return a16

    total = jnp.zeros((variables, points), F32)
    weights, contexts = {}, {}
    for step in range(groups + 2):
        if step < groups:
            weights[step] = attend(step)
        if 0 <= step - 1 < groups:
            contexts[step - 1] = jnp.dot(vt[step - 1], weights[step - 1], preferred_element_type=F32).astype(BF16)
        if 0 <= step - 2:
            g = step - 2
            total = total + jnp.dot(wo[:, pl.ds(g * GROUP, GROUP)], contexts[g], preferred_element_type=F32)
    pred[pl.ds(0, variables), :] = total

    pl.semaphore_wait(hello_one, 4)
    for k in order:
        send(pred.at[pl.ds(pl.multiple_of(peers[k] * ROWS, ROWS), ROWS)], got.at[k],
             go_send, go_recv, peers[k], region)
    first = pl.multiple_of(me * ROWS, ROWS)
    got[0] = pred[pl.ds(first, ROWS), :]
    drain(got.at[pl.ds(1, members - 1)], go_send)
    drain(got.at[pl.ds(1, members - 1)], go_recv)
    pl.semaphore_wait(hello_two, CORES * ((rz >= 2).astype(jnp.int32) + (rz < deep - 2).astype(jnp.int32)))
    along(hello_four, lax.rem(rz + 4, deep))

    coeff = 1.0 - (1.0 - ALPHA) / members
    pair = coeff / (members * (members - 1))
    loss_part = jnp.zeros((8, 128), F32)
    for top in range(0, ROWS, 8):
        row = lax.broadcasted_iota(jnp.int32, (8, 128), 0) + first + top
        valid = row < variables
        block_loss = jnp.zeros((8, 128), F32)
        for left in range(0, points, 128):
            at = (pl.ds(top, 8), pl.ds(left, 128))
            goal = tpad[pl.ds(first + top, 8), pl.ds(left, 128)]
            ps = [got[(k,) + at] for k in range(members)]
            slopes = [None] * members
            near = jnp.zeros((8, 128), F32)
            apart = jnp.full((8, 128), 0.5 * members * math.sqrt(DELTA_SQ), F32)
            grads = []
            for i in range(members):
                d = ps[i] - goal
                sq = d * d + DELTA_SQ
                inv = lax.rsqrt(sq)
                near = near + sq * inv
                grads.append(d * inv)
            for i in range(members):
                for j in range(i + 1, members):
                    d = ps[i] - ps[j]
                    sq = d * d + DELTA_SQ
                    inv = lax.rsqrt(sq)
                    apart = apart + sq * inv
                    d = d * inv
                    slopes[i] = d if slopes[i] is None else slopes[i] + d
                    slopes[j] = -d if slopes[j] is None else slopes[j] - d
            block_loss = block_loss + (near * (1.0 / members) - apart * pair)
            for i in range(members):
                back_out[(i,) + at] = (grads[i] * (1.0 / members) - slopes[i] * pair).astype(BF16)
        loss_part = loss_part + jnp.where(valid, block_loss, 0.0)

    loss_part = jnp.sum(loss_part, axis=0, keepdims=True)
    mine[0] = loss_part
    slot = rx * tall + ry
    plane_loss[slot] = loss_part
    for _, m, r in plane:
        send(mine.at[0], plane_loss.at[slot], pl_send, pl_recv, m, r)
    for k in order:
        owner = lax.rem(me + members - k, members)
        send(back_out.at[k], back.at[pl.ds(first, ROWS)], ret_send, ret_recv, owner, region)
    back[pl.ds(first, ROWS), :] = back_out[0]

    drain(plane_loss.at[pl.ds(1, len(plane))], pl_send)
    drain(plane_loss.at[pl.ds(1, len(plane))], pl_recv)
    pl.semaphore_wait(hello_four, CORES)
    loss_part = plane_loss[0]
    for k in range(1, wide * tall):
        loss_part = loss_part + plane_loss[k]
    loss_part = jnp.broadcast_to(jnp.sum(loss_part, axis=1, keepdims=True) * (1.0 / npts), loss_part.shape)
    mine[1] = loss_part
    slot = rz * CORES + rc
    deep_loss[slot] = loss_part
    for _, m, r in line:
        send(mine.at[1], deep_loss.at[slot], dl_send, dl_recv, m, r)

    drain(back_out.at[pl.ds(1, members - 1)], ret_send)
    drain(back_out.at[pl.ds(1, members - 1)], ret_recv)
    gcs, gas, gk, gv = [], [], [], []
    for g in range(groups):
        gc = jnp.dot(won[pl.ds(g * GROUP, GROUP), :], back[...], preferred_element_type=F32).astype(BF16)
        gcs.append(gc)
    for g in range(groups):
        gas.append(jnp.dot(vbd[g], gcs[g], preferred_element_type=F32))
    for g in range(groups):
        gv.append(gather(lax.dot_general(attn16[g], gcs[g], NT, preferred_element_type=F32)).astype(BF16))
    for g in range(groups):
        cols = pl.ds(g * GROUP, GROUP)
        ga = gas[g]
        parts, rim_parts = [], []
        for h in range(heads):
            at = stacked + h * 2 * HALO
            a, f = attn[g, pl.ds(h * own_nodes, own_nodes), :], attn[g, pl.ds(at, 2 * HALO), :]
            t, u = a * ga[h * own_nodes : (h + 1) * own_nodes], f * ga[at : at + 2 * HALO]
            mean = fold(jnp.add, jnp.sum, t, u)
            parts.append(t - a * mean)
            rim_parts.append(u - f * mean)
        gs = jnp.concatenate(parts + rim_parts, axis=0).astype(BF16)
        gk.append((gather(jnp.dot(gs, query[:, cols], preferred_element_type=F32)) * scale).astype(BF16))
    gk = jnp.concatenate(gk, axis=1)
    gv = jnp.concatenate(gv, axis=1)

    for c in range(width // GROUP):
        cols = pl.ds(c * GROUP, GROUP)
        out = lax.dot_general(gk, wk[cols, :], NT, preferred_element_type=F32)
        out = out + lax.dot_general(gv, wv[cols, :], NT, preferred_element_type=F32)
        gl[:, cols] = out[own_nodes:]
        grad_out[:, cols] = out[:own_nodes]
    rims = swap(
        gl.at[pl.ds(0, HALO)], halo.at[1], gl.at[pl.ds(HALO, HALO)], halo.at[0], (halo_send, halo_recv)
    )
    rims()
    grad_out[pl.ds(0, HALO), :] += halo[0]
    grad_out[pl.ds(own_nodes - HALO, HALO), :] += halo[1]

    drain(deep_loss.at[pl.ds(1, len(line))], dl_send)
    drain(deep_loss.at[pl.ds(1, len(line))], dl_recv)
    loss_part = deep_loss[0]
    for k in range(1, deep * CORES):
        loss_part = loss_part + deep_loss[k]
    loss_out[...] = jnp.broadcast_to(loss_part, loss_out.shape)


def finish(grad, loss, grad_out, loss_out, one, sem):
    copies = [pltpu.make_async_copy(grad, grad_out, sem.at[0]), pltpu.make_async_copy(one, loss_out, sem.at[1])]
    copies[0].start()
    one[...] = loss[pl.ds(0, 1), pl.ds(0, 1)]
    copies[1].start()
    for copy in copies:
        copy.wait()


def local(members, regions, mesh_latent, grid_feat, edges, target, w_query, w_key, w_value, w_out):
    latent = mesh_latent[0]
    feats = grid_feat[0]
    own_nodes, width = latent.shape
    points, links = edges.shape
    variables = target.shape[1]
    window = own_nodes + 2 * HALO
    deep = math.gcd(regions, 8) if regions > 8 else 2
    wide, tall = regions // deep, members // CORES
    groups = width // GROUP
    stack = window * GROUP // (width // HEADS)
    padded = members * ROWS
    dma = pltpu.SemaphoreType.DMA
    any_space = pl.BlockSpec(memory_space=pltpu.HBM)
    vmem = pl.BlockSpec(memory_space=pltpu.VMEM)
    grad, loss = pl.pallas_call(
        functools.partial(kernel, members, regions, deep, points * regions * variables),
        out_shape=(
            jax.ShapeDtypeStruct((own_nodes, width), F32),
            jax.ShapeDtypeStruct((8, 128), F32),
        ),
        in_specs=[any_space] * 8,
        out_specs=(vmem, vmem),
        scratch_shapes=[
            pltpu.VMEM((own_nodes, width), BF16),
            pltpu.VMEM((points, width), BF16),
            pltpu.VMEM((links, points), jnp.int32),
            pltpu.VMEM((variables, points), F32),
            pltpu.VMEM((width, width), BF16),
            pltpu.VMEM((width, width), BF16),
            pltpu.VMEM((width, width), BF16),
            pltpu.VMEM((variables, width), BF16),
            pltpu.VMEM((2, own_nodes, width), F32),
            pltpu.VMEM((2, 2 * HALO, width), BF16),
            pltpu.VMEM((2, 2 * HALO, width), BF16),
            pltpu.VMEM((padded, points), F32),
            pltpu.VMEM((padded, width), F32),
            pltpu.VMEM((width, padded), BF16),
            pltpu.VMEM((points, width), BF16),
            pltpu.VMEM((groups, stack, points), F32),
            pltpu.VMEM((HEADS, 1, points), F32),
            pltpu.VMEM((HEADS, 1, points), F32),
            pltpu.VMEM((groups, GROUP, stack), BF16),
            pltpu.VMEM((groups, stack, GROUP), BF16),
            pltpu.VMEM((groups, stack, points), F32),
            pltpu.VMEM((groups, stack, points), BF16),
            pltpu.VMEM((padded, points), F32),
            pltpu.VMEM((members, ROWS, points), F32),
            pltpu.VMEM((members, ROWS, points), BF16),
            pltpu.VMEM((padded, points), BF16),
            pltpu.VMEM((2 * HALO, width), F32),
            pltpu.VMEM((2, HALO, width), F32),
            pltpu.VMEM((wide * tall, 1, 128), F32),
            pltpu.VMEM((deep * CORES, 1, 128), F32),
            pltpu.VMEM((2, 1, 128), F32),
            pltpu.SemaphoreType.REGULAR,
            pltpu.SemaphoreType.REGULAR,
            pltpu.SemaphoreType.REGULAR,
            dma((8,)),
            dma((2,)), dma((2,)),
            dma, dma,
            dma, dma,
            dma((2,)), dma((2,)),
            dma, dma,
            dma, dma,
        ],
        compiler_params=pltpu.CompilerParams(
            collective_id=0, has_side_effects=True, vmem_limit_bytes=24 * 1024 * 1024
        ),
    )(*[pltpu.with_memory_space_constraint(x, pltpu.HBM) for x in (latent, feats, edges.T, target.T, w_query, w_key, w_value, w_out.T)])
    grad, loss = pl.pallas_call(
        finish,
        out_shape=(
            jax.ShapeDtypeStruct((own_nodes, width), F32),
            jax.ShapeDtypeStruct((1, 1), F32),
        ),
        in_specs=[vmem, vmem],
        out_specs=(pl.BlockSpec(memory_space=pltpu.HBM), pl.BlockSpec(memory_space=pltpu.HBM)),
        scratch_shapes=[pltpu.VMEM((1, 1), F32), dma((2,))],
        compiler_params=pltpu.CompilerParams(vmem_limit_bytes=4 * 1024 * 1024),
    )(grad, loss)
    return grad[None], loss[0, 0]


def solution(mesh):
    in_specs = (
        P("ens", "grid", None),
        P("ens", "grid", None),
        P("grid", None),
        P("grid", None),
        P(),
        P(),
        P(),
        P(),
    )
    out_specs = (P("ens", "grid", None), P())
    return jax.shard_map(
        functools.partial(local, mesh.shape["ens"], mesh.shape["grid"]),
        mesh=mesh, in_specs=in_specs, out_specs=out_specs, check_vma=False,
    )
```
